256 devices in a mesh: aa: 8 (over x, y_hi), ba: 32 (over z, y_lo, core).
Axes of the slice: x: 4, y: 4 (y_hi: 2, y_lo: 2; y = y_hi * 2 + y_lo), z: 8, core: 2. Of those that a mesh axis runs over, the one named last changes fastest.
Arguments:
- ligand_slab: bfloat16 [64, 128, 16384], P(None, 'aa', 'ba'), may hold values from -6 to 6
- protein_slab: bfloat16 [64, 1024, 16384], P(None, 'ba', 'aa'), may hold values from -6 to 6
- protein_orbitals: bfloat16 [1024, 16384], P(None, 'ba'), may hold values from -0.046875 to 0.046875
- ligand_orbitals: bfloat16 [128, 16384], P(None, 'aa'), may hold values from -0.046875 to 0.046875
Outputs:
- pair_exchange: float32 [128, 1024], P('aa', 'ba')
- ligand_back: float32 [16384, 128], P(('aa', 'ba'))
- protein_back: float32 [16384, 1024], P(('ba', 'aa'))
The draws below stay inside these ranges and needn't reach their ends.
All inputs are finite; a program needn't handle non-finite values.
Results may differ from the reference program's by a relative error of at most 0.0024.
Values may be sent and summed in bfloat16 or wider, within the bound.
No kernel may reach another device: no remote copies, remote signals or barrier semaphores. Data moves between devices by JAX's collectives and lax.ppermute only.
A program may use at most 192 MiB of HBM per device.

```python
import math
import jax
import jax.numpy as jnp
from jax import lax

NQ = 64
NA = 128
NB = 1024
NBF = 16384


def level_of(key, dims, shards, smallest, largest):
    def one(position, shards_of):
        heights = jax.random.uniform(jax.random.fold_in(jax.random.fold_in(key, 6), position), (shards_of,), jnp.float32, smallest / len(shards), largest / len(shards))
        return jnp.repeat(jnp.exp(heights), dims[position] // shards_of).reshape((-1,) + (1,) * (len(dims) - position - 1))

    loudness = one(*shards[0])
    for cut in shards[1:]:
        loudness = loudness * one(*cut)
    return loudness


def bell_draw(own_key, extent, width, reach, shards=(), kind=jnp.bfloat16):
    array = jax.random.normal(own_key, extent, jnp.float32) * width
    if len(shards) > 0:
        array = level_of(own_key, extent, shards, -0.22, 0.18) * array
    return jnp.clip(array, min=-reach, max=reach).astype(kind)


def setup_inputs(seed: int = 0) -> dict:
    arg_keys = jax.random.split(jax.random.key(seed), 5)
    return {
        "ligand_slab": bell_draw(arg_keys[0], (NQ, NA, NBF), 1.0, 6.0, ((1, 8), (2, 32))),
        "protein_slab": bell_draw(arg_keys[1], (NQ, NB, NBF), 1.0, 6.0, ((1, 32), (2, 8))),
        "protein_orbitals": bell_draw(arg_keys[2], (NB, NBF), NBF ** -0.5, 0.046875, ((1, 32),)),
        "ligand_orbitals": bell_draw(arg_keys[3], (NA, NBF), NBF ** -0.5, 0.046875, ((1, 8),)),
    }


def reference(ligand_slab, protein_slab, protein_orbitals, ligand_orbitals):

    def advance(carry, slabs):
        pair_sum, ligand_acc, protein_acc = carry
        lig_rows, pro_rows = slabs
        cross_a = jnp.dot(lig_rows, protein_orbitals.T, preferred_element_type=jnp.float32)
        cross_b = jnp.dot(ligand_orbitals, pro_rows.T, preferred_element_type=jnp.float32)
        pair_sum = pair_sum + cross_a * cross_b
        rounded_a = cross_a.astype(jnp.bfloat16)
        rounded_b = cross_b.astype(jnp.bfloat16)
        protein_acc = protein_acc + jnp.dot(lig_rows.T, rounded_a, preferred_element_type=jnp.float32)
        ligand_acc = ligand_acc + jnp.dot(pro_rows.T, rounded_b.T, preferred_element_type=jnp.float32)
        return ((pair_sum, ligand_acc, protein_acc), None)
    start_state = (jnp.zeros((NA, NB), jnp.float32), jnp.zeros((NBF, NA), jnp.float32), jnp.zeros((NBF, NB), jnp.float32))
    final_state, _ = lax.scan(advance, start_state, (ligand_slab, protein_slab))
    pair_sum, ligand_acc, protein_acc = final_state
    pair_exchange = -pair_sum / math.sqrt(NQ)
    ligand_back = ligand_acc / math.sqrt(NQ * NB)
    protein_back = protein_acc / math.sqrt(NQ * NA)
    return (pair_exchange, ligand_back, protein_back)
```

```python
import math

import jax
import jax.numpy as jnp
from jax import lax
from jax.sharding import Mesh, PartitionSpec as P

AXES = ("x", "yh", "z", "yl", "c")
AA = ("x", "yh")
ZY = ("z", "yl")
F32 = jnp.float32
BF16 = jnp.bfloat16


def flat_perm(sizes, shift):
    first, second = sizes
    return [
        (i * second + j, ((i + shift[0]) % first) * second + (j + shift[1]) % second)
        for i in range(first)
        for j in range(second)
    ]


def shifts(sizes):
    return [(i, j) for i in range(sizes[0]) for j in range(sizes[1]) if (i, j) != (0, 0)]


def scatter_sum(pieces, axes, sizes):
    me = [lax.axis_index(name) for name in axes]
    total = lax.dynamic_index_in_dim(pieces, me[0] * sizes[1] + me[1], 0, keepdims=False)
    for shift in shifts(sizes):
        target = lax.rem(me[0] + shift[0], sizes[0]) * sizes[1] + lax.rem(me[1] + shift[1], sizes[1])
        piece = lax.dynamic_index_in_dim(pieces, target, 0, keepdims=False)
        total = total + lax.ppermute(piece, axes, flat_perm(sizes, shift))
    return total


def scatter_sum_all(pieces, axes):
    return jnp.sum(lax.all_to_all(pieces, axes, 0, 0, tiled=True), axis=0)


def gather(block, axes, sizes):
    me = [lax.axis_index(name) for name in axes]
    out = jnp.zeros((sizes[0] * sizes[1],) + block.shape, block.dtype)
    out = lax.dynamic_update_index_in_dim(out, block, me[0] * sizes[1] + me[1], 0)
    for shift in shifts(sizes):
        source = lax.rem(me[0] + sizes[0] - shift[0], sizes[0]) * sizes[1] + lax.rem(
            me[1] + sizes[1] - shift[1], sizes[1]
        )
        got = lax.ppermute(block, axes, flat_perm(sizes, shift))
        out = lax.dynamic_update_index_in_dim(out, got, source, 0)
    return out


def swap(block):
    return lax.ppermute(block, "c", [(0, 1), (1, 0)])


def dot(left, right, contract):
    return lax.dot_general(left, right, (contract, ((), ())), preferred_element_type=F32)


def on_device(ligand_slab, protein_slab, protein_orbitals, ligand_orbitals, *, sizes):
    aa = tuple(sizes[name] for name in AA)
    zy = tuple(sizes[name] for name in ZY)
    n_aa, n_zy = aa[0] * aa[1], zy[0] * zy[1]
    fit, lig, mus = ligand_slab.shape
    _, pro, nus = protein_slab.shape
    lig_total, pro_total = ligand_orbitals.shape[0], protein_orbitals.shape[0]
    core = lax.axis_index("c")

    x_own = ligand_slab.reshape(fit * lig, mus)
    y = protein_slab.reshape(fit * pro, nus)
    orb = protein_orbitals.reshape(n_zy, 2, pro, mus)
    orb_own = lax.dynamic_index_in_dim(orb, core, 1, keepdims=False).reshape(n_zy * pro, mus)
    orb_send = lax.dynamic_index_in_dim(orb, 1 - core, 1, keepdims=False).reshape(n_zy * pro, mus)
    x_other = swap(x_own)
    orb_other = swap(orb_send)

    b_part = dot(ligand_orbitals, y, ((1,), (1,)))
    b_own = scatter_sum(b_part.reshape(n_aa, lig, fit * pro), AA, aa)

    a_part = dot(orb_own, x_own, ((1,), (1,))) + dot(orb_other, x_other, ((1,), (1,)))
    a_own = scatter_sum_all(a_part.reshape(n_zy, pro, fit * lig), ZY)

    b_all = gather(b_own.astype(BF16), AA, aa).reshape(n_aa * lig, fit * pro)
    a_all = gather(a_own.astype(BF16), ZY, zy).reshape(n_zy * pro, fit * lig)

    pair = jnp.sum(
        jnp.transpose(a_own.reshape(pro, fit, lig), (1, 2, 0))
        * jnp.transpose(b_own.reshape(lig, fit, pro), (1, 0, 2)),
        axis=0,
    )
    pair_exchange = -pair / math.sqrt(fit)

    scale_ligand = 1.0 / math.sqrt(fit * pro_total)
    back_b = dot(y, b_all, ((0,), (1,))) * scale_ligand
    back_b = back_b.reshape(n_zy, 2, nus // (2 * n_zy), lig_total)
    keep = lax.dynamic_index_in_dim(back_b, core, 1, keepdims=False)
    send = lax.dynamic_index_in_dim(back_b, 1 - core, 1, keepdims=False)
    ligand_back = scatter_sum_all(keep + swap(send), ZY)

    scale_protein = 1.0 / math.sqrt(fit * lig_total)
    half = n_zy * pro
    back_other = dot(x_other, a_all, ((0,), (1,))) * scale_protein
    back_own = dot(x_own, a_all, ((0,), (1,))) * scale_protein
    away = scatter_sum_all(back_other.reshape(n_aa, mus // n_aa, half), AA)
    here = scatter_sum_all(back_own.reshape(n_aa, mus // n_aa, half), AA)
    there = swap(away)
    rows = mus // n_aa
    here = here.reshape(rows, n_zy, 1, pro)
    there = there.reshape(rows, n_zy, 1, pro)
    protein_back = jnp.where(
        core == 0,
        jnp.concatenate([here, there], axis=2),
        jnp.concatenate([there, here], axis=2),
    ).reshape(rows, pro_total)
    return (pair_exchange, ligand_back, protein_back)


def solution(mesh):
    sizes = {"x": mesh.shape["aa"] // 2, "yh": 2, "z": mesh.shape["ba"] // 4, "yl": 2, "c": 2}
    fine = Mesh(mesh.devices.reshape([sizes[name] for name in AXES]), AXES)
    aa, ba = AA, ("z", "yl", "c")
    placed = (P(None, aa, ba), P(None, ba, aa), P(None, ba), P(None, aa))

    def body(*args):
        return on_device(*args, sizes=sizes)

    return jax.shard_map(
        body,
        mesh=fine,
        in_specs=placed,
        out_specs=(P(aa, ba), P(aa + ba, None), P(ba + aa, None)),
        check_vma=False,
    )
```

```python
import math

import jax
import jax.numpy as jnp
from jax import lax
from jax.sharding import Mesh, PartitionSpec as P

AXES = ("x", "yh", "z", "yl", "c")
AA = ("x", "yh")
ZY = ("z", "yl")
F32 = jnp.float32
F16 = jnp.float16
BF16 = jnp.bfloat16
LANES = 128


def exchange(pieces, axes):
    return lax.all_to_all(pieces, axes, 0, 0, tiled=True)


def scatter_sum(pieces, axes):
    return jnp.sum(exchange(pieces, axes).astype(F32), axis=0)


def gather(block, axes, count):
    return exchange(jnp.broadcast_to(block[None], (count,) + block.shape), axes)


def swap(block):
    return lax.ppermute(block, "c", [(0, 1), (1, 0)])


def dot(left, right, contract):
    return lax.dot_general(left, right, (contract, ((), ())), preferred_element_type=F32)


def largest(*arrays):
    tops = [jnp.max(jnp.abs(array)).astype(F32) for array in arrays]
    return jnp.maximum(*tops)


def on_device(ligand_slab, protein_slab, protein_orbitals, ligand_orbitals, *, sizes):
    n_aa = sizes["x"] * sizes["yh"]
    n_zy = sizes["z"] * sizes["yl"]
    fit, lig, mus = ligand_slab.shape
    _, pro, nus = protein_slab.shape
    lig_total, pro_total = ligand_orbitals.shape[0], protein_orbitals.shape[0]
    core = lax.axis_index("c")
    wide = fit * lig

    x_own = ligand_slab.reshape(wide, mus)
    y = protein_slab.reshape(fit * pro, nus)
    orb = protein_orbitals.reshape(n_zy, 2, pro, mus)
    orb_own = lax.dynamic_index_in_dim(orb, core, 1, keepdims=False).reshape(n_zy * pro, mus)
    orb_send = lax.dynamic_index_in_dim(orb, 1 - core, 1, keepdims=False).reshape(n_zy * pro, mus)
    orb_other = swap(orb_send)
    x_other = swap(x_own)

    a_part = dot(orb_own, x_own, ((1,), (1,))) + dot(orb_other, x_other, ((1,), (1,)))
    bound = (2.0 * mus) * largest(x_own, x_other) * largest(orb_own, orb_other)
    code = jnp.ceil(jnp.log2(jnp.maximum(bound, 1e-30))) + 1.0
    a_sent = (a_part * jnp.exp2(15.0 - code)).astype(F16)
    a_sent = jnp.concatenate([a_sent, jnp.broadcast_to(code.astype(F16), (n_zy * pro, LANES))], axis=1)
    a_got = exchange(a_sent.reshape(n_zy, pro, wide + LANES), ZY)
    codes = a_got[:, :1, wide : wide + 1].astype(F32)
    a_own = jnp.sum(a_got[:, :, :wide].astype(F32) * jnp.exp2(codes - 15.0), axis=0)
    a_all = gather(a_own.astype(BF16), ZY, n_zy).reshape(n_zy * pro, wide)

    b_part = dot(ligand_orbitals, y, ((1,), (1,)))
    b_own = scatter_sum(b_part.reshape(n_aa, lig, fit * pro), AA)
    b_all = gather(b_own.astype(BF16), AA, n_aa).reshape(n_aa * lig, fit * pro)

    pair = jnp.sum(
        jnp.transpose(a_own.reshape(pro, fit, lig), (1, 2, 0))
        * jnp.transpose(b_own.reshape(lig, fit, pro), (1, 0, 2)),
        axis=0,
    )
    pair_exchange = -pair / math.sqrt(fit)

    scale_ligand = 1.0 / math.sqrt(fit * pro_total)
    back_b = dot(y, b_all, ((0,), (1,))) * scale_ligand
    back_b = back_b.reshape(n_zy, 2, nus // (2 * n_zy), lig_total)
    keep = lax.dynamic_index_in_dim(back_b, core, 1, keepdims=False)
    send = lax.dynamic_index_in_dim(back_b, 1 - core, 1, keepdims=False)
    ligand_back = scatter_sum((keep + swap(send)).astype(BF16), ZY)

    scale_protein = 1.0 / math.sqrt(fit * lig_total)
    half = n_zy * pro
    rows = mus // n_aa
    x_chip = jnp.stack(
        [x_own.T.reshape(n_aa, rows, wide), x_other.T.reshape(n_aa, rows, wide)], axis=1
    ).reshape(2 * mus, wide)
    back_a = (dot(x_chip, a_all, ((1,), (1,))) * scale_protein).astype(BF16)
    here, away = scatter_sum(back_a.reshape(n_aa, 2, rows, half), AA)
    there = swap(away)
    here = here.reshape(rows, n_zy, 1, pro)
    there = there.reshape(rows, n_zy, 1, pro)
    protein_back = jnp.where(
        core == 0,
        jnp.concatenate([here, there], axis=2),
        jnp.concatenate([there, here], axis=2),
    ).reshape(rows, pro_total)
    return (pair_exchange, ligand_back, protein_back)


def solution(mesh):
    sizes = {"x": mesh.shape["aa"] // 2, "yh": 2, "z": mesh.shape["ba"] // 4, "yl": 2, "c": 2}
    fine = Mesh(mesh.devices.reshape([sizes[name] for name in AXES]), AXES)
    aa, ba = AA, ("z", "yl", "c")
    placed = (P(None, aa, ba), P(None, ba, aa), P(None, ba), P(None, aa))

    def body(*args):
        return on_device(*args, sizes=sizes)

    return jax.shard_map(
        body,
        mesh=fine,
        in_specs=placed,
        out_specs=(P(aa, ba), P(aa + ba, None), P(ba + aa, None)),
        check_vma=False,
    )
```

```python
import math

import jax
import jax.numpy as jnp
from jax import lax
from jax.sharding import Mesh, PartitionSpec as P

AXES = ("x", "yh", "z", "yl", "c")
AA = ("x", "yh")
F32 = jnp.float32
BF16 = jnp.bfloat16


def exchange(pieces, axes):
    return lax.all_to_all(pieces, axes, 0, 0, tiled=True)


def scatter_sum(pieces, axes):
    return jnp.sum(exchange(pieces, axes).astype(F32), axis=0)


def gather(block, axes, count):
    return exchange(jnp.broadcast_to(block[None], (count,) + block.shape), axes)


def dot(left, right, contract):
    return lax.dot_general(left, right, (contract, ((), ())), preferred_element_type=F32)


def pick(pieces, index, count):
    return lax.dynamic_index_in_dim(pieces, lax.rem(index + count, count), 0, keepdims=False)


def ring_sum(pieces, axis, count):
    me = lax.axis_index(axis)
    up = [(i, (i + 1) % count) for i in range(count)]
    down = [(i, (i - 1) % count) for i in range(count)]
    far = count // 2
    mid = pieces.shape[1] // 2
    away = pick(pieces, me + far, count)
    right = lax.ppermute(away[:mid], axis, up)
    left = lax.ppermute(away[mid:], axis, down)
    for hop in range(far - 1, 0, -1):
        to_right = pick(pieces, me + hop, count)
        to_left = pick(pieces, me - hop, count)
        if hop == far - 1:
            to_right = jnp.concatenate([to_right[:mid] + right, to_right[mid:]], axis=0)
            to_left = jnp.concatenate([to_left[:mid], to_left[mid:] + left], axis=0)
        else:
            to_right = to_right + right
            to_left = to_left + left
        right = lax.ppermute(to_right, axis, up)
        left = lax.ppermute(to_left, axis, down)
    return pick(pieces, me, count) + (right + left)


def ring_gather(block, axis, count):
    me = lax.axis_index(axis)
    up = [(i, (i + 1) % count) for i in range(count)]
    down = [(i, (i - 1) % count) for i in range(count)]
    far = count // 2
    mid = block.shape[0] // 2
    out = jnp.zeros((count,) + block.shape, block.dtype)

    def put(out, part, index):
        return lax.dynamic_update_index_in_dim(out, part, lax.rem(index + count, count), 0)

    out = put(out, block, me)
    right = left = block
    for hop in range(1, far):
        right = lax.ppermute(right, axis, up)
        left = lax.ppermute(left, axis, down)
        out = put(out, right, me - hop)
        out = put(out, left, me + hop)
    right = lax.ppermute(right[:mid], axis, up)
    left = lax.ppermute(left[mid:], axis, down)
    return put(out, jnp.concatenate([right, left], axis=0), me + far)


def other(block, axis):
    return lax.ppermute(block, axis, [(0, 1), (1, 0)])


def pair_sum(pieces, axis):
    me = lax.axis_index(axis)
    keep = lax.dynamic_index_in_dim(pieces, me, 1, keepdims=False)
    send = lax.dynamic_index_in_dim(pieces, 1 - me, 1, keepdims=False)
    return keep + other(send, axis)


def pair_gather(block, axis):
    got = other(block, axis)
    return jnp.where(lax.axis_index(axis) == 0, jnp.stack([block, got]), jnp.stack([got, block]))


def on_device(ligand_slab, protein_slab, protein_orbitals, ligand_orbitals, *, sizes):
    n_aa = sizes["x"] * sizes["yh"]
    n_z = sizes["z"]
    n_zy = n_z * sizes["yl"]
    fit, lig, mus = ligand_slab.shape
    _, pro, nus = protein_slab.shape
    lig_total, pro_total = ligand_orbitals.shape[0], protein_orbitals.shape[0]
    core = lax.axis_index("c")
    wide = fit * lig

    x_own = ligand_slab.reshape(wide, mus)
    y = protein_slab.reshape(fit * pro, nus)
    orb = protein_orbitals.reshape(n_zy, 2, pro, mus)
    orb_own = lax.dynamic_index_in_dim(orb, core, 1, keepdims=False).reshape(n_zy * pro, mus)
    orb_send = lax.dynamic_index_in_dim(orb, 1 - core, 1, keepdims=False).reshape(n_zy * pro, mus)
    orb_other = other(orb_send, "c")
    x_other = other(x_own, "c")

    a_part = dot(orb_own, x_own, ((1,), (1,))) + dot(orb_other, x_other, ((1,), (1,)))
    a_z = ring_sum(a_part.reshape(n_z, 2 * pro, wide), "z", n_z)
    a_own = pair_sum(a_z.reshape(1, 2, pro, wide), "yl").reshape(pro, wide)
    a_pair = pair_gather(a_own.astype(BF16), "yl").reshape(2 * pro, wide)
    a_all = ring_gather(a_pair, "z", n_z).reshape(n_zy * pro, wide)

    b_part = dot(ligand_orbitals, y, ((1,), (1,)))
    b_own = scatter_sum(b_part.reshape(n_aa, lig, fit * pro), AA)
    b_all = gather(b_own.astype(BF16), AA, n_aa).reshape(n_aa * lig, fit * pro)

    pair = jnp.sum(
        jnp.transpose(a_own.reshape(pro, fit, lig), (1, 2, 0))
        * jnp.transpose(b_own.reshape(lig, fit, pro), (1, 0, 2)),
        axis=0,
    )
    pair_exchange = -pair / math.sqrt(fit)

    scale_ligand = 1.0 / math.sqrt(fit * pro_total)
    back_b = dot(y, b_all, ((0,), (1,))) * scale_ligand
    rows_b = nus // (2 * n_zy)
    back_b = pair_sum(back_b.reshape(n_zy, 2, rows_b, lig_total), "c")
    back_b = ring_sum(back_b.reshape(n_z, 2 * rows_b, lig_total), "z", n_z)
    ligand_back = pair_sum(back_b.reshape(1, 2, rows_b, lig_total), "yl").reshape(rows_b, lig_total)

    scale_protein = 1.0 / math.sqrt(fit * lig_total)
    half = n_zy * pro
    rows = mus // n_aa
    x_chip = jnp.stack(
        [x_own.T.reshape(n_aa, rows, wide), x_other.T.reshape(n_aa, rows, wide)], axis=1
    ).reshape(2 * mus, wide)
    back_a = (dot(x_chip, a_all, ((1,), (1,))) * scale_protein).astype(BF16)
    here, away = scatter_sum(back_a.reshape(n_aa, 2, rows, half), AA)
    there = other(away, "c")
    here = here.reshape(rows, n_zy, 1, pro)
    there = there.reshape(rows, n_zy, 1, pro)
    protein_back = jnp.where(
        core == 0,
        jnp.concatenate([here, there], axis=2),
        jnp.concatenate([there, here], axis=2),
    ).reshape(rows, pro_total)
    return (pair_exchange, ligand_back, protein_back)


def solution(mesh):
    sizes = {"x": mesh.shape["aa"] // 2, "yh": 2, "z": mesh.shape["ba"] // 4, "yl": 2, "c": 2}
    fine = Mesh(mesh.devices.reshape([sizes[name] for name in AXES]), AXES)
    aa, ba = AA, ("z", "yl", "c")
    placed = (P(None, aa, ba), P(None, ba, aa), P(None, ba), P(None, aa))

    def body(*args):
        return on_device(*args, sizes=sizes)

    return jax.shard_map(
        body,
        mesh=fine,
        in_specs=placed,
        out_specs=(P(aa, ba), P(aa + ba, None), P(ba + aa, None)),
        check_vma=False,
    )
```

```python
import itertools
import math

import jax
import jax.numpy as jnp
from jax import lax
from jax.sharding import Mesh, PartitionSpec as P

AXES = ("x", "yh", "z", "yl", "c")
AA = ("x", "yh")
ZY = ("z", "yl")
F32 = jnp.float32
F16 = jnp.float16
BF16 = jnp.bfloat16
LANES = 128


def exchange(pieces, axes):
    return lax.all_to_all(pieces, axes, 0, 0, tiled=True)


def shifts(sizes):
    return list(itertools.product(*(range(size) for size in sizes)))[1:]


def flat(place, sizes):
    index = 0
    for part, size in zip(place, sizes):
        index = index * size + part
    return index


def moved(sizes, shift):
    places = itertools.product(*(range(size) for size in sizes))
    return [
        (flat(place, sizes), flat([(p + s) % n for p, s, n in zip(place, shift, sizes)], sizes))
        for place in places
    ]


def peer(axes, sizes, shift):
    return flat(
        [lax.rem(lax.axis_index(name) + s, n) for name, s, n in zip(axes, shift, sizes)], sizes
    )


def direct_sum(pieces, axes, sizes):
    own = (0,) * len(sizes)
    total = lax.dynamic_index_in_dim(pieces, peer(axes, sizes, own), 0, keepdims=False).astype(F32)
    for shift in shifts(sizes):
        piece = lax.dynamic_index_in_dim(pieces, peer(axes, sizes, shift), 0, keepdims=False)
        total = total + lax.ppermute(piece, axes, moved(sizes, shift)).astype(F32)
    return total


def direct_gather(block, axes, sizes):
    own = (0,) * len(sizes)
    out = jnp.zeros((math.prod(sizes),) + block.shape, block.dtype)
    out = lax.dynamic_update_index_in_dim(out, block, peer(axes, sizes, own), 0)
    for shift in shifts(sizes):
        got = lax.ppermute(block, axes, moved(sizes, shift))
        back = [n - s for s, n in zip(shift, sizes)]
        out = lax.dynamic_update_index_in_dim(out, got, peer(axes, sizes, back), 0)
    return out


def other(block, axis):
    return lax.ppermute(block, axis, [(0, 1), (1, 0)])


def pair_sum(pieces, axis):
    me = lax.axis_index(axis)
    keep = lax.dynamic_index_in_dim(pieces, me, 1, keepdims=False)
    send = lax.dynamic_index_in_dim(pieces, 1 - me, 1, keepdims=False)
    return keep + other(send, axis)


def after(array, done):
    return array + (0.0 * done[:1, :1].astype(F32)).astype(array.dtype)


def dot(left, right, contract):
    return lax.dot_general(left, right, (contract, ((), ())), preferred_element_type=F32)


def largest(array):
    return jnp.max(jnp.abs(array)).astype(F32)


def on_device(ligand_slab, protein_slab, protein_orbitals, ligand_orbitals, *, sizes):
    aa = (sizes["x"], sizes["yh"])
    n_aa = aa[0] * aa[1]
    n_z, n_yl = sizes["z"], sizes["yl"]
    n_zy = n_z * n_yl
    fit, lig, mus = ligand_slab.shape
    _, pro, nus = protein_slab.shape
    lig_total, pro_total = ligand_orbitals.shape[0], protein_orbitals.shape[0]
    core = lax.axis_index("c")
    wide = fit * lig

    x_own = ligand_slab.reshape(wide, mus)
    y = protein_slab.reshape(fit * pro, nus)
    x_other = other(x_own, "c")
    orb = protein_orbitals.reshape(n_zy, 2, pro, mus)
    orb_own = lax.dynamic_index_in_dim(orb, core, 1, keepdims=False).reshape(n_zy * pro, mus)
    orb_send = lax.dynamic_index_in_dim(orb, 1 - core, 1, keepdims=False).reshape(n_zy * pro, mus)
    orb_other = other(orb_send, "c")

    tops = jnp.broadcast_to(
        jnp.stack([largest(x_own), largest(protein_orbitals)])[:, None], (2, LANES)
    )
    tops = jnp.maximum(tops, other(tops, "c"))[:, 0]
    bound = (2.0 * mus) * tops[0] * tops[1]
    code = jnp.ceil(jnp.log2(jnp.maximum(bound, 1e-30))) + 1.0
    a_part = dot(orb_own, x_own, ((1,), (1,))) + dot(orb_other, x_other, ((1,), (1,)))
    a_sent = (a_part * jnp.exp2(15.0 - code)).astype(F16)
    a_sent = jnp.concatenate([a_sent, jnp.broadcast_to(code.astype(F16), (n_zy * pro, LANES))], axis=1)
    a_got = exchange(a_sent.reshape(n_zy, pro, wide + LANES), ZY)
    codes = a_got[:, :1, wide : wide + 1].astype(F32)
    a_own = jnp.sum(a_got[:, :, :wide].astype(F32) * jnp.exp2(codes - 15.0), axis=0)
    a_block = jnp.broadcast_to(a_own.astype(BF16)[None], (n_zy, pro, wide))
    a_all = exchange(a_block, ZY).reshape(n_zy * pro, wide)

    b_part = dot(after(ligand_orbitals, a_sent), y, ((1,), (1,))).astype(BF16)
    b_own = direct_sum(b_part.reshape(n_aa, lig, fit * pro), AA, aa)
    b_block = after(b_own, a_own).astype(BF16)
    b_all = direct_gather(b_block, AA, aa).reshape(n_aa * lig, fit * pro)

    pair = jnp.sum(
        jnp.transpose(a_own.reshape(pro, fit, lig), (1, 2, 0))
        * jnp.transpose(b_own.reshape(lig, fit, pro), (1, 0, 2)),
        axis=0,
    )
    pair_exchange = -pair / math.sqrt(fit)

    scale_ligand = 1.0 / math.sqrt(fit * pro_total)
    rows_b = nus // (2 * n_zy)
    back_b = dot(y, b_all, ((0,), (1,))) * scale_ligand
    back_b = pair_sum(back_b.reshape(n_zy, 2, rows_b, lig_total), "c")
    back_b = pair_sum(back_b.reshape(n_z, n_yl, rows_b, lig_total), "yl")
    back_b = after(back_b.reshape(n_z * rows_b, lig_total), a_all)
    ligand_back = direct_sum(back_b.reshape(n_z, rows_b, lig_total), ("z",), (n_z,))

    scale_protein = 1.0 / math.sqrt(fit * lig_total)
    half = n_zy * pro
    rows = mus // n_aa
    x_chip = jnp.stack(
        [x_own.T.reshape(n_aa, rows, wide), x_other.T.reshape(n_aa, rows, wide)], axis=1
    ).reshape(2 * mus, wide)
    back_a = (dot(x_chip, a_all, ((1,), (1,))) * scale_protein).astype(BF16)
    back_a = exchange(back_a.reshape(n_aa, 2, rows, half), AA)
    here, away = jnp.sum(back_a.astype(F32), axis=0)
    there = other(away, "c")
    here = here.reshape(rows, n_zy, 1, pro)
    there = there.reshape(rows, n_zy, 1, pro)
    protein_back = jnp.where(
        core == 0,
        jnp.concatenate([here, there], axis=2),
        jnp.concatenate([there, here], axis=2),
    ).reshape(rows, pro_total)
    return (pair_exchange, ligand_back, protein_back)


def solution(mesh):
    sizes = {"x": mesh.shape["aa"] // 2, "yh": 2, "z": mesh.shape["ba"] // 4, "yl": 2, "c": 2}
    fine = Mesh(mesh.devices.reshape([sizes[name] for name in AXES]), AXES)
    aa, ba = AA, ("z", "yl", "c")
    placed = (P(None, aa, ba), P(None, ba, aa), P(None, ba), P(None, aa))

    def body(*args):
        return on_device(*args, sizes=sizes)

    return jax.shard_map(
        body,
        mesh=fine,
        in_specs=placed,
        out_specs=(P(aa, ba), P(aa + ba, None), P(ba + aa, None)),
        check_vma=False,
    )
```

```python
import itertools
import math

import jax
import jax.numpy as jnp
from jax import lax
from jax.experimental import pallas as pl
from jax.experimental.pallas import tpu as pltpu
from jax.sharding import Mesh, PartitionSpec as P

AXES = ("x", "yh", "z", "yl", "c")
AA = ("x", "yh")
ZY = ("z", "yl")
F32 = jnp.float32
F16 = jnp.float16
BF16 = jnp.bfloat16
LANES = 128
VMEM = 54 * 2**20


def exchange(pieces, axes):
    return lax.all_to_all(pieces, axes, 0, 0, tiled=True)


def shifts(sizes):
    return list(itertools.product(*(range(size) for size in sizes)))[1:]


def flat(place, sizes):
    index = 0
    for part, size in zip(place, sizes):
        index = index * size + part
    return index


def moved(sizes, shift):
    places = itertools.product(*(range(size) for size in sizes))
    return [
        (flat(place, sizes), flat([(p + s) % n for p, s, n in zip(place, shift, sizes)], sizes))
        for place in places
    ]


def peer(axes, sizes, shift):
    return flat(
        [lax.rem(lax.axis_index(name) + s, n) for name, s, n in zip(axes, shift, sizes)], sizes
    )


def direct_sum(pieces, axes, sizes):
    own = (0,) * len(sizes)
    total = lax.dynamic_index_in_dim(pieces, peer(axes, sizes, own), 0, keepdims=False).astype(F32)
    for shift in shifts(sizes):
        piece = lax.dynamic_index_in_dim(pieces, peer(axes, sizes, shift), 0, keepdims=False)
        total = total + lax.ppermute(piece, axes, moved(sizes, shift)).astype(F32)
    return total


def direct_gather(block, axes, sizes):
    blocks, places = [block], [peer(axes, sizes, (0,) * len(sizes))]
    for shift in shifts(sizes):
        blocks.append(lax.ppermute(block, axes, moved(sizes, shift)))
        places.append(peer(axes, sizes, [n - s for s, n in zip(shift, sizes)]))
    return blocks, places


def other(block, axis):
    return lax.ppermute(block, axis, [(0, 1), (1, 0)])


def pair_sum(pieces, axis):
    me = lax.axis_index(axis)
    keep = lax.dynamic_index_in_dim(pieces, me, 1, keepdims=False)
    send = lax.dynamic_index_in_dim(pieces, 1 - me, 1, keepdims=False)
    return keep + other(send, axis)


def dot(left, right, contract):
    return lax.dot_general(left, right, (contract, ((), ())), preferred_element_type=F32)


def largest(array):
    return jnp.max(jnp.abs(array)).astype(F32)


def cross_kernel(token_ref, left_ref, right_ref, out_ref):
    del token_ref
    out_ref[...] = dot(left_ref[...], right_ref[...], ((1,), (1,))).astype(out_ref.dtype)


def cross_part(token, orbitals, slab):
    rows, depth = slab.shape
    step = min(rows, 256)
    return pl.pallas_call(
        cross_kernel,
        grid=(rows // step,),
        in_specs=[
            pl.BlockSpec(token.shape, lambda i: (0, 0)),
            pl.BlockSpec(orbitals.shape, lambda i: (0, 0)),
            pl.BlockSpec((step, depth), lambda i: (i, 0)),
        ],
        out_specs=pl.BlockSpec((orbitals.shape[0], step), lambda i: (0, i)),
        out_shape=jax.ShapeDtypeStruct((orbitals.shape[0], rows), BF16),
        compiler_params=pltpu.CompilerParams(vmem_limit_bytes=VMEM),
        cost_estimate=pl.CostEstimate(flops=0, bytes_accessed=0, transcendentals=0),
        name="cross_part",
    )(token, orbitals, slab)


def back_kernel(place_ref, slab_ref, *refs, count, scale, fine):
    blocks, (keep_ref, send_ref, all_ref) = refs[:count], refs[count:]

    @pl.when(pl.program_id(0) == 0)
    def _():
        for k, block_ref in enumerate(blocks):
            rows = block_ref.shape[0]
            all_ref[pl.ds(pl.multiple_of(place_ref[k] * rows, rows), rows), :] = block_ref[...]

    part = dot(all_ref[...], slab_ref[...], ((1,), (0,))) * scale
    part = part.T.reshape(-1, 2, fine, all_ref.shape[0])
    first, second = part[:, 0], part[:, 1]
    low = place_ref[count] == 0
    keep_ref[...] = jnp.where(low, first, second)
    send_ref[...] = jnp.where(low, second, first)


def back_part(slab, blocks, places, core, scale, fine):
    count = len(blocks)
    depth, total = slab.shape
    rows = blocks[0].shape[0]
    step = min(total, 256)
    out = pl.BlockSpec((step // (2 * fine), fine, count * rows), lambda i, _: (i, 0, 0))
    shape = jax.ShapeDtypeStruct((total // (2 * fine), fine, count * rows), F32)
    return pl.pallas_call(
        lambda *refs: back_kernel(*refs, count=count, scale=scale, fine=fine),
        grid_spec=pltpu.PrefetchScalarGridSpec(
            num_scalar_prefetch=1,
            grid=(total // step,),
            in_specs=[pl.BlockSpec((depth, step), lambda i, _: (0, i))]
            + [pl.BlockSpec((rows, depth), lambda i, _: (0, 0))] * count,
            out_specs=[out, out],
            scratch_shapes=[pltpu.VMEM((count * rows, depth), BF16)],
        ),
        out_shape=[shape, shape],
        compiler_params=pltpu.CompilerParams(vmem_limit_bytes=VMEM),
        cost_estimate=pl.CostEstimate(flops=0, bytes_accessed=0, transcendentals=0),
        name="back_part",
    )(jnp.stack(places + [core]).astype(jnp.int32), slab, *blocks)


def spread_kernel(token_ref, block_ref, out_ref):
    del token_ref
    out_ref[...] = jnp.broadcast_to(block_ref[...].astype(out_ref.dtype)[None], out_ref.shape)


def spread(token, block, count):
    return pl.pallas_call(
        spread_kernel,
        grid=(1,),
        in_specs=[
            pl.BlockSpec((8, LANES), lambda i: (0, 0)),
            pl.BlockSpec(block.shape, lambda i: (0, 0)),
        ],
        out_specs=pl.BlockSpec((count,) + block.shape, lambda i: (0, 0, 0)),
        out_shape=jax.ShapeDtypeStruct((count,) + block.shape, BF16),
        cost_estimate=pl.CostEstimate(flops=0, bytes_accessed=0, transcendentals=0),
        name="spread",
    )(token, block)


def product_kernel(token_ref, left_ref, right_ref, out_ref, *, scale):
    del token_ref
    part = dot(left_ref[...], right_ref[...], ((1,), (1,))) * scale
    out_ref[...] = part.astype(out_ref.dtype)


def product(token, left, right, scale):
    rows, depth = left.shape
    step = min(rows, 256)
    return pl.pallas_call(
        lambda *refs: product_kernel(*refs, scale=scale),
        grid=(rows // step,),
        in_specs=[
            pl.BlockSpec((8, LANES), lambda i: (0, 0)),
            pl.BlockSpec((step, depth), lambda i: (i, 0)),
            pl.BlockSpec(right.shape, lambda i: (0, 0)),
        ],
        out_specs=pl.BlockSpec((step, right.shape[0]), lambda i: (i, 0)),
        out_shape=jax.ShapeDtypeStruct((rows, right.shape[0]), BF16),
        cost_estimate=pl.CostEstimate(flops=0, bytes_accessed=0, transcendentals=0),
        name="product",
    )(token, left, right)


def on_device(ligand_slab, protein_slab, protein_orbitals, ligand_orbitals, *, sizes):
    aa = (sizes["x"], sizes["yh"])
    n_aa = aa[0] * aa[1]
    n_z, n_yl = sizes["z"], sizes["yl"]
    n_zy = n_z * n_yl
    fit, lig, mus = ligand_slab.shape
    _, pro, nus = protein_slab.shape
    lig_total, pro_total = ligand_orbitals.shape[0], protein_orbitals.shape[0]
    core = lax.axis_index("c")
    wide = fit * lig

    x_own = ligand_slab.reshape(wide, mus)
    y = protein_slab.reshape(fit * pro, nus)
    x_other = other(x_own, "c")
    orb = protein_orbitals.reshape(n_zy, 2, pro, mus)
    orb_own = lax.dynamic_index_in_dim(orb, core, 1, keepdims=False).reshape(n_zy * pro, mus)
    orb_send = lax.dynamic_index_in_dim(orb, 1 - core, 1, keepdims=False).reshape(n_zy * pro, mus)
    orb_other = other(orb_send, "c")

    tops = jnp.broadcast_to(
        jnp.stack([largest(x_own), largest(protein_orbitals)])[:, None], (2, LANES)
    )
    tops = jnp.maximum(tops, other(tops, "c"))[:, 0]
    bound = (2.0 * mus) * tops[0] * tops[1]
    code = jnp.ceil(jnp.log2(jnp.maximum(bound, 1e-30))) + 1.0
    a_part = dot(orb_own, x_own, ((1,), (1,))) + dot(orb_other, x_other, ((1,), (1,)))
    a_sent = (a_part * jnp.exp2(15.0 - code)).astype(F16)
    a_sent = jnp.concatenate([a_sent, jnp.broadcast_to(code.astype(F16), (n_zy * pro, LANES))], axis=1)
    a_got = exchange(a_sent.reshape(n_zy, pro, wide + LANES), ZY)
    codes = a_got[:, :1, wide : wide + 1].astype(F32)
    a_own = jnp.sum(a_got[:, :, :wide].astype(F32) * jnp.exp2(codes - 15.0), axis=0)

    b_part = cross_part(a_sent[:8, :LANES].astype(F32), ligand_orbitals, y)
    b_own = direct_sum(b_part.reshape(n_aa, lig, fit * pro), AA, aa)
    a_all = exchange(spread(b_own, a_own, n_zy), ZY).reshape(n_zy * pro, wide)
    b_blocks, b_places = direct_gather(b_own.astype(BF16), AA, aa)

    pair = jnp.sum(
        jnp.transpose(a_own.reshape(pro, fit, lig), (1, 2, 0))
        * jnp.transpose(b_own.reshape(lig, fit, pro), (1, 0, 2)),
        axis=0,
    )
    pair_exchange = -pair / math.sqrt(fit)

    scale_ligand = 1.0 / math.sqrt(fit * pro_total)
    rows_b = nus // (2 * n_zy)
    keep, send = back_part(y, b_blocks, b_places, core, scale_ligand, rows_b)
    back_b = keep + other(send, "c")
    ligand_back = direct_sum(back_b.reshape(n_z, n_yl * rows_b, lig_total), ("z",), (n_z,))
    ligand_back = pair_sum(ligand_back.reshape(1, n_yl, rows_b, lig_total), "yl").reshape(rows_b, lig_total)

    scale_protein = 1.0 / math.sqrt(fit * lig_total)
    half = n_zy * pro
    rows = mus // n_aa
    x_chip = jnp.stack(
        [x_own.T.reshape(n_aa, rows, wide), x_other.T.reshape(n_aa, rows, wide)], axis=1
    ).reshape(2 * mus, wide)
    back_a = product(back_b.reshape(n_zy * rows_b, lig_total), x_chip, a_all, scale_protein)
    back_a = exchange(back_a.reshape(n_aa, 2, rows, half), AA)
    here, away = jnp.sum(back_a.astype(F32), axis=0)
    there = other(away, "c")
    here = here.reshape(rows, n_zy, 1, pro)
    there = there.reshape(rows, n_zy, 1, pro)
    protein_back = jnp.where(
        core == 0,
        jnp.concatenate([here, there], axis=2),
        jnp.concatenate([there, here], axis=2),
    ).reshape(rows, pro_total)
    return (pair_exchange, ligand_back, protein_back)


def solution(mesh):
    sizes = {"x": mesh.shape["aa"] // 2, "yh": 2, "z": mesh.shape["ba"] // 4, "yl": 2, "c": 2}
    fine = Mesh(mesh.devices.reshape([sizes[name] for name in AXES]), AXES)
    aa, ba = AA, ("z", "yl", "c")
    placed = (P(None, aa, ba), P(None, ba, aa), P(None, ba), P(None, aa))

    def body(*args):
        return on_device(*args, sizes=sizes)

    return jax.shard_map(
        body,
        mesh=fine,
        in_specs=placed,
        out_specs=(P(aa, ba), P(aa + ba, None), P(ba + aa, None)),
        check_vma=False,
    )
```

```python
import itertools
import math

import jax
import jax.numpy as jnp
from jax import lax
from jax.experimental import pallas as pl
from jax.experimental.pallas import tpu as pltpu
from jax.sharding import Mesh, PartitionSpec as P

AXES = ("x", "yh", "z", "yl", "c")
AA = ("x", "yh")
ZY = ("z", "yl")
F32 = jnp.float32
F16 = jnp.float16
BF16 = jnp.bfloat16
LANES = 128
VMEM = 24 * 2**20


def exchange(pieces, axes):
    return lax.all_to_all(pieces, axes, 0, 0, tiled=True)


def shifts(sizes):
    return list(itertools.product(*(range(size) for size in sizes)))[1:]


def flat(place, sizes):
    index = 0
    for part, size in zip(place, sizes):
        index = index * size + part
    return index


def moved(sizes, shift):
    places = itertools.product(*(range(size) for size in sizes))
    return [
        (flat(place, sizes), flat([(p + s) % n for p, s, n in zip(place, shift, sizes)], sizes))
        for place in places
    ]


def peer(axes, sizes, shift):
    return flat(
        [lax.rem(lax.axis_index(name) + s, n) for name, s, n in zip(axes, shift, sizes)], sizes
    )


def direct_sum(pieces, axes, sizes, sent):
    own = (0,) * len(sizes)
    total = lax.dynamic_index_in_dim(pieces, peer(axes, sizes, own), 0, keepdims=False).astype(F32)
    for shift in shifts(sizes):
        piece = lax.dynamic_index_in_dim(pieces, peer(axes, sizes, shift), 0, keepdims=False)
        total = total + lax.ppermute(piece.astype(sent), axes, moved(sizes, shift)).astype(F32)
    return total


def direct_gather(block, axes, sizes):
    blocks, places = [block], [peer(axes, sizes, (0,) * len(sizes))]
    for shift in shifts(sizes):
        blocks.append(lax.ppermute(block, axes, moved(sizes, shift)))
        places.append(peer(axes, sizes, [n - s for s, n in zip(shift, sizes)]))
    return blocks, places


def other(block, axis):
    return lax.ppermute(block, axis, [(0, 1), (1, 0)])


def pair_sum(pieces, axis):
    me = lax.axis_index(axis)
    keep = lax.dynamic_index_in_dim(pieces, me, 1, keepdims=False)
    send = lax.dynamic_index_in_dim(pieces, 1 - me, 1, keepdims=False)
    return keep + other(send, axis)


def dot(left, right, contract):
    return lax.dot_general(left, right, (contract, ((), ())), preferred_element_type=F32)


def largest(array):
    return jnp.max(jnp.abs(array)).astype(F32)


def cross_kernel(token_ref, left_ref, slab_ref, out_ref, held_ref, sems, *, step):
    del token_ref
    copies = []
    for i in range(held_ref.shape[0] // step):
        rows = pl.ds(i * step, step)
        copies.append(pltpu.make_async_copy(slab_ref.at[rows], held_ref.at[rows], sems.at[i]))
        copies[i].start()
    for i, copy in enumerate(copies):
        rows = pl.ds(i * step, step)
        copy.wait()
        part = dot(left_ref[...], held_ref[rows, :], ((1,), (1,)))
        out_ref[:, rows] = part.astype(out_ref.dtype)


def cross_part(token, orbitals, slab):
    rows = slab.shape[0]
    step = min(rows, 256)
    return pl.pallas_call(
        lambda *refs: cross_kernel(*refs, step=step),
        in_specs=[
            pl.BlockSpec(memory_space=pltpu.VMEM),
            pl.BlockSpec(memory_space=pltpu.VMEM),
            pl.BlockSpec(memory_space=pltpu.HBM),
        ],
        out_specs=pl.BlockSpec(memory_space=pltpu.VMEM),
        out_shape=jax.ShapeDtypeStruct((orbitals.shape[0], rows), BF16),
        scratch_shapes=[pltpu.VMEM(slab.shape, BF16), pltpu.SemaphoreType.DMA((rows // step,))],
        compiler_params=pltpu.CompilerParams(vmem_limit_bytes=VMEM),
        cost_estimate=pl.CostEstimate(flops=0, bytes_accessed=0, transcendentals=0),
        name="cross_part",
    )(token, orbitals, slab)


def back_kernel(place_ref, slab_ref, *refs, count, scale, fine, step):
    blocks, (keep_ref, send_ref, all_ref, held_ref, sems) = refs[:count], refs[count:]
    copies = []
    for i in range(held_ref.shape[0]):
        columns = pl.ds(i * step, step)
        copies.append(pltpu.make_async_copy(slab_ref.at[:, columns], held_ref.at[i], sems.at[i]))
        copies[i].start()
    for k, block_ref in enumerate(blocks):
        rows = block_ref.shape[0]
        all_ref[pl.ds(pl.multiple_of(place_ref[k] * rows, rows), rows), :] = block_ref[...]
    low = place_ref[count] == 0
    runs = step // (2 * fine)
    for i, copy in enumerate(copies):
        copy.wait()
        part = dot(all_ref[...], held_ref[i], ((1,), (0,))) * scale
        part = part.T.reshape(runs, 2, fine, all_ref.shape[0])
        first, second = part[:, 0], part[:, 1]
        keep_ref[pl.ds(i * runs, runs)] = jnp.where(low, first, second)
        send_ref[pl.ds(i * runs, runs)] = jnp.where(low, second, first)


def back_part(slab, blocks, places, core, scale, fine):
    count = len(blocks)
    depth, total = slab.shape
    rows = blocks[0].shape[0]
    step = min(total, 256)
    shape = jax.ShapeDtypeStruct((total // (2 * fine), fine, count * rows), F32)
    whole = pl.BlockSpec(memory_space=pltpu.VMEM)
    return pl.pallas_call(
        lambda *refs: back_kernel(*refs, count=count, scale=scale, fine=fine, step=step),
        in_specs=[pl.BlockSpec(memory_space=pltpu.SMEM), pl.BlockSpec(memory_space=pltpu.HBM)]
        + [whole] * count,
        out_specs=[whole, whole],
        out_shape=[shape, shape],
        scratch_shapes=[
            pltpu.VMEM((count * rows, depth), BF16),
            pltpu.VMEM((total // step, depth, step), BF16),
            pltpu.SemaphoreType.DMA((total // step,)),
        ],
        compiler_params=pltpu.CompilerParams(vmem_limit_bytes=VMEM),
        cost_estimate=pl.CostEstimate(flops=0, bytes_accessed=0, transcendentals=0),
        name="back_part",
    )(jnp.stack(places + [core]).astype(jnp.int32), slab, *blocks)


def spread_kernel(token_ref, block_ref, out_ref):
    del token_ref
    out_ref[...] = jnp.broadcast_to(block_ref[...].astype(out_ref.dtype)[None], out_ref.shape)


def spread(token, block, count):
    return pl.pallas_call(
        spread_kernel,
        grid=(1,),
        in_specs=[
            pl.BlockSpec((8, LANES), lambda i: (0, 0)),
            pl.BlockSpec(block.shape, lambda i: (0, 0)),
        ],
        out_specs=pl.BlockSpec((count,) + block.shape, lambda i: (0, 0, 0)),
        out_shape=jax.ShapeDtypeStruct((count,) + block.shape, BF16),
        cost_estimate=pl.CostEstimate(flops=0, bytes_accessed=0, transcendentals=0),
        name="spread",
    )(token, block)


def product_kernel(token_ref, own_ref, other_ref, right_ref, out_ref, *, scale, step):
    del token_ref
    runs = step // out_ref.shape[2]
    for i in range(own_ref.shape[1] // step):
        columns = pl.ds(i * step, step)
        for k, left_ref in enumerate((own_ref, other_ref)):
            part = dot(right_ref[...], left_ref[:, columns], ((1,), (0,))) * scale
            part = part.T.reshape(runs, out_ref.shape[2], right_ref.shape[0])
            out_ref[pl.ds(i * runs, runs), k] = part.astype(out_ref.dtype)


def product(token, own, other_core, right, scale, fine):
    total = own.shape[1]
    step = min(total, 256)
    whole = pl.BlockSpec(memory_space=pltpu.VMEM)
    return pl.pallas_call(
        lambda *refs: product_kernel(*refs, scale=scale, step=step),
        grid=(1,),
        in_specs=[pl.BlockSpec((8, LANES), lambda i: (0, 0)), whole, whole, whole],
        out_specs=whole,
        out_shape=jax.ShapeDtypeStruct((total // fine, 2, fine, right.shape[0]), BF16),
        compiler_params=pltpu.CompilerParams(vmem_limit_bytes=VMEM),
        cost_estimate=pl.CostEstimate(flops=0, bytes_accessed=0, transcendentals=0),
        name="product",
    )(token, own, other_core, right)


def on_device(ligand_slab, protein_slab, protein_orbitals, ligand_orbitals, *, sizes):
    aa = (sizes["x"], sizes["yh"])
    n_aa = aa[0] * aa[1]
    n_z, n_yl = sizes["z"], sizes["yl"]
    n_zy = n_z * n_yl
    fit, lig, mus = ligand_slab.shape
    _, pro, nus = protein_slab.shape
    lig_total, pro_total = ligand_orbitals.shape[0], protein_orbitals.shape[0]
    core = lax.axis_index("c")
    wide = fit * lig

    x_own = ligand_slab.reshape(wide, mus)
    y = protein_slab.reshape(fit * pro, nus)
    x_other = other(x_own, "c")
    orb = protein_orbitals.reshape(n_zy, 2, pro, mus)
    orb_own = lax.dynamic_index_in_dim(orb, core, 1, keepdims=False).reshape(n_zy * pro, mus)
    orb_send = lax.dynamic_index_in_dim(orb, 1 - core, 1, keepdims=False).reshape(n_zy * pro, mus)
    orb_other = other(orb_send, "c")

    tops = jnp.stack([largest(x_own), largest(protein_orbitals)])
    tops = jnp.broadcast_to(tops[:, None], (2, wide + LANES))
    tops = jnp.maximum(tops, other(tops, "c"))
    bound = (2.0 * mus) * tops[:1] * tops[1:]
    code = jnp.ceil(jnp.log2(jnp.maximum(bound, 1e-30))) + 1.0
    a_part = dot(orb_own, x_own, ((1,), (1,))) + dot(orb_other, x_other, ((1,), (1,)))
    a_sent = (a_part * jnp.exp2(15.0 - code[:, :wide])).astype(F16)
    code = jnp.broadcast_to(code[:, wide:].astype(F16), (n_zy * pro, LANES))
    a_sent = jnp.concatenate([a_sent, code], axis=1)
    a_got = exchange(a_sent.reshape(n_zy, pro, wide + LANES), ZY)
    codes = a_got[:, :1, wide : wide + 1].astype(F32)
    a_own = jnp.sum(a_got[:, :, :wide].astype(F32) * jnp.exp2(codes - 15.0), axis=0)

    b_part = cross_part(a_sent[:8, :LANES].astype(F32), ligand_orbitals, y)
    b_own = direct_sum(b_part.reshape(n_aa, lig, fit * pro), AA, aa, BF16)
    a_all = exchange(spread(b_own, a_own, n_zy), ZY).reshape(n_zy * pro, wide)
    b_blocks, b_places = direct_gather(b_own.astype(BF16), AA, aa)

    pair = jnp.sum(
        jnp.transpose(a_own.reshape(pro, fit, lig), (1, 2, 0))
        * jnp.transpose(b_own.reshape(lig, fit, pro), (1, 0, 2)),
        axis=0,
    )
    pair_exchange = -pair / math.sqrt(fit)

    scale_ligand = 1.0 / math.sqrt(fit * pro_total)
    rows_b = nus // (2 * n_zy)
    keep, send = back_part(y, b_blocks, b_places, core, scale_ligand, rows_b)
    back_b = keep + other(send, "c")
    ligand_back = direct_sum(back_b.reshape(n_z, n_yl * rows_b, lig_total), ("z",), (n_z,), BF16)
    ligand_back = pair_sum(ligand_back.reshape(1, n_yl, rows_b, lig_total), "yl").reshape(rows_b, lig_total)

    scale_protein = 1.0 / math.sqrt(fit * lig_total)
    rows = mus // n_aa
    token = back_b.reshape(n_zy * rows_b, lig_total)
    back_a = product(token, x_own, x_other, a_all, scale_protein, rows)
    back_a = exchange(back_a, AA)
    here, away = jnp.sum(back_a.astype(F32), axis=0)
    there = other(away, "c")
    here = here.reshape(rows, n_zy, 1, pro)
    there = there.reshape(rows, n_zy, 1, pro)
    protein_back = jnp.where(
        core == 0,
        jnp.concatenate([here, there], axis=2),
        jnp.concatenate([there, here], axis=2),
    ).reshape(rows, pro_total)
    return (pair_exchange, ligand_back, protein_back)


def solution(mesh):
    sizes = {"x": mesh.shape["aa"] // 2, "yh": 2, "z": mesh.shape["ba"] // 4, "yl": 2, "c": 2}
    fine = Mesh(mesh.devices.reshape([sizes[name] for name in AXES]), AXES)
    aa, ba = AA, ("z", "yl", "c")
    placed = (P(None, aa, ba), P(None, ba, aa), P(None, ba), P(None, aa))

    def body(*args):
        return on_device(*args, sizes=sizes)

    return jax.shard_map(
        body,
        mesh=fine,
        in_specs=placed,
        out_specs=(P(aa, ba), P(aa + ba, None), P(ba + aa, None)),
        check_vma=False,
    )
```

```python
import itertools
import math

import jax
import jax.numpy as jnp
from jax import lax
from jax.experimental import pallas as pl
from jax.experimental.pallas import tpu as pltpu
from jax.sharding import Mesh, PartitionSpec as P

AXES = ("x", "yh", "z", "yl", "c")
AA = ("x", "yh")
ZY = ("z", "yl")
F32 = jnp.float32
F16 = jnp.float16
BF16 = jnp.bfloat16
LANES = 128
VMEM = 24 * 2**20
LARGE = 54 * 2**20
DEEP = 3


def exchange(pieces, axes):
    return lax.all_to_all(pieces, axes, 0, 0, tiled=True)


def shifts(sizes):
    return list(itertools.product(*(range(size) for size in sizes)))[1:]


def flat(place, sizes):
    index = 0
    for part, size in zip(place, sizes):
        index = index * size + part
    return index


def moved(sizes, shift):
    places = itertools.product(*(range(size) for size in sizes))
    return [
        (flat(place, sizes), flat([(p + s) % n for p, s, n in zip(place, shift, sizes)], sizes))
        for place in places
    ]


def peer(axes, sizes, shift):
    return flat(
        [lax.rem(lax.axis_index(name) + s, n) for name, s, n in zip(axes, shift, sizes)], sizes
    )


def direct_sum(pieces, axes, sizes, sent):
    own = (0,) * len(sizes)
    total = lax.dynamic_index_in_dim(pieces, peer(axes, sizes, own), 0, keepdims=False).astype(F32)
    for shift in shifts(sizes):
        piece = lax.dynamic_index_in_dim(pieces, peer(axes, sizes, shift), 0, keepdims=False)
        total = total + lax.ppermute(piece.astype(sent), axes, moved(sizes, shift)).astype(F32)
    return total


def direct_gather(block, axes, sizes):
    blocks, places = [block], [peer(axes, sizes, (0,) * len(sizes))]
    for shift in shifts(sizes):
        blocks.append(lax.ppermute(block, axes, moved(sizes, shift)))
        places.append(peer(axes, sizes, [n - s for s, n in zip(shift, sizes)]))
    return blocks, places


def other(block, axis):
    return lax.ppermute(block, axis, [(0, 1), (1, 0)])


def pair_sum(pieces, axis):
    me = lax.axis_index(axis)
    keep = lax.dynamic_index_in_dim(pieces, me, 1, keepdims=False)
    send = lax.dynamic_index_in_dim(pieces, 1 - me, 1, keepdims=False)
    return keep + other(send, axis)


def dot(left, right, contract):
    return lax.dot_general(left, right, (contract, ((), ())), preferred_element_type=F32)


def largest(array):
    return jnp.max(jnp.abs(array)).astype(F32)


def arriving(copies):
    for copy in copies[:DEEP]:
        copy.start()
    for i, copy in enumerate(copies):
        copy.wait()
        if i + DEEP < len(copies):
            copies[i + DEEP].start()
        yield i


def cross_kernel(left_ref, slab_ref, out_ref, held_ref, sems, *, step):
    runs = [pl.ds(i * step, step) for i in range(held_ref.shape[0] // step)]
    copies = [
        pltpu.make_async_copy(slab_ref.at[rows], held_ref.at[rows], sems.at[i])
        for i, rows in enumerate(runs)
    ]
    for i in arriving(copies):
        part = dot(left_ref[...], held_ref[runs[i], :], ((1,), (1,)))
        out_ref[:, runs[i]] = part.astype(out_ref.dtype)


def cross_part(orbitals, slab):
    rows = slab.shape[0]
    step = min(rows, 256)
    return pl.pallas_call(
        lambda *refs: cross_kernel(*refs, step=step),
        in_specs=[pl.BlockSpec(memory_space=pltpu.VMEM), pl.BlockSpec(memory_space=pltpu.HBM)],
        out_specs=pl.BlockSpec(memory_space=pltpu.VMEM),
        out_shape=jax.ShapeDtypeStruct((orbitals.shape[0], rows), BF16),
        scratch_shapes=[pltpu.VMEM(slab.shape, BF16), pltpu.SemaphoreType.DMA((rows // step,))],
        compiler_params=pltpu.CompilerParams(vmem_limit_bytes=LARGE),
        cost_estimate=pl.CostEstimate(flops=0, bytes_accessed=0, transcendentals=0),
        name="cross_part",
    )(orbitals, slab)


def back_kernel(place_ref, slab_ref, *refs, count, scale, fine, step):
    blocks, (keep_ref, send_ref, all_ref, held_ref, sems) = refs[:count], refs[count:]
    copies = [
        pltpu.make_async_copy(slab_ref.at[:, pl.ds(i * step, step)], held_ref.at[i], sems.at[i])
        for i in range(held_ref.shape[0])
    ]
    for k, block_ref in enumerate(blocks):
        rows = block_ref.shape[0]
        all_ref[pl.ds(pl.multiple_of(place_ref[k] * rows, rows), rows), :] = block_ref[...]
    low = place_ref[count] == 0
    runs = step // (2 * fine)
    for i in arriving(copies):
        part = dot(all_ref[...], held_ref[i], ((1,), (0,))) * scale
        part = part.T.reshape(runs, 2, fine, all_ref.shape[0])
        first, second = part[:, 0], part[:, 1]
        keep_ref[pl.ds(i * runs, runs)] = jnp.where(low, first, second)
        send_ref[pl.ds(i * runs, runs)] = jnp.where(low, second, first)


def back_part(slab, blocks, places, core, scale, fine):
    count = len(blocks)
    depth, total = slab.shape
    rows = blocks[0].shape[0]
    step = min(total, 256)
    shape = jax.ShapeDtypeStruct((total // (2 * fine), fine, count * rows), F32)
    whole = pl.BlockSpec(memory_space=pltpu.VMEM)
    return pl.pallas_call(
        lambda *refs: back_kernel(*refs, count=count, scale=scale, fine=fine, step=step),
        in_specs=[pl.BlockSpec(memory_space=pltpu.SMEM), pl.BlockSpec(memory_space=pltpu.HBM)]
        + [whole] * count,
        out_specs=[whole, whole],
        out_shape=[shape, shape],
        scratch_shapes=[
            pltpu.VMEM((count * rows, depth), BF16),
            pltpu.VMEM((total // step, depth, step), BF16),
            pltpu.SemaphoreType.DMA((total // step,)),
        ],
        compiler_params=pltpu.CompilerParams(vmem_limit_bytes=LARGE),
        cost_estimate=pl.CostEstimate(flops=0, bytes_accessed=0, transcendentals=0),
        name="back_part",
    )(jnp.stack(places + [core]).astype(jnp.int32), slab, *blocks)


def spread_kernel(token_ref, block_ref, out_ref):
    del token_ref
    out_ref[...] = jnp.broadcast_to(block_ref[...].astype(out_ref.dtype)[None], out_ref.shape)


def spread(token, block, count):
    return pl.pallas_call(
        spread_kernel,
        grid=(1,),
        in_specs=[
            pl.BlockSpec((8, LANES), lambda i: (0, 0)),
            pl.BlockSpec(block.shape, lambda i: (0, 0)),
        ],
        out_specs=pl.BlockSpec((count,) + block.shape, lambda i: (0, 0, 0)),
        out_shape=jax.ShapeDtypeStruct((count,) + block.shape, BF16),
        cost_estimate=pl.CostEstimate(flops=0, bytes_accessed=0, transcendentals=0),
        name="spread",
    )(token, block)


def product_kernel(token_ref, own_ref, other_ref, right_ref, out_ref, *, scale, step):
    del token_ref
    runs = step // out_ref.shape[2]
    for i in range(own_ref.shape[1] // step):
        columns = pl.ds(i * step, step)
        for k, left_ref in enumerate((own_ref, other_ref)):
            part = dot(right_ref[...], left_ref[:, columns], ((1,), (0,))) * scale
            part = part.T.reshape(runs, out_ref.shape[2], right_ref.shape[0])
            out_ref[pl.ds(i * runs, runs), k] = part.astype(out_ref.dtype)


def product(token, own, other_core, right, scale, fine):
    total = own.shape[1]
    step = min(total, 256)
    whole = pl.BlockSpec(memory_space=pltpu.VMEM)
    return pl.pallas_call(
        lambda *refs: product_kernel(*refs, scale=scale, step=step),
        grid=(1,),
        in_specs=[pl.BlockSpec((8, LANES), lambda i: (0, 0)), whole, whole, whole],
        out_specs=whole,
        out_shape=jax.ShapeDtypeStruct((total // fine, 2, fine, right.shape[0]), BF16),
        compiler_params=pltpu.CompilerParams(vmem_limit_bytes=VMEM),
        cost_estimate=pl.CostEstimate(flops=0, bytes_accessed=0, transcendentals=0),
        name="product",
    )(token, own, other_core, right)


def on_device(ligand_slab, protein_slab, protein_orbitals, ligand_orbitals, *, sizes):
    aa = (sizes["x"], sizes["yh"])
    n_aa = aa[0] * aa[1]
    n_z, n_yl = sizes["z"], sizes["yl"]
    n_zy = n_z * n_yl
    fit, lig, mus = ligand_slab.shape
    _, pro, nus = protein_slab.shape
    lig_total, pro_total = ligand_orbitals.shape[0], protein_orbitals.shape[0]
    core = lax.axis_index("c")
    wide = fit * lig

    x_own = ligand_slab.reshape(wide, mus)
    y = protein_slab.reshape(fit * pro, nus)
    x_other = other(x_own, "c")
    orb = protein_orbitals.reshape(n_zy, 2, pro, mus)
    orb_own = lax.dynamic_index_in_dim(orb, core, 1, keepdims=False).reshape(n_zy * pro, mus)
    orb_send = lax.dynamic_index_in_dim(orb, 1 - core, 1, keepdims=False).reshape(n_zy * pro, mus)
    orb_other = other(orb_send, "c")

    b_part = cross_part(ligand_orbitals, y)
    b_own = jnp.sum(exchange(b_part.reshape(n_aa, lig, fit * pro), AA).astype(F32), axis=0)

    tops = jnp.stack([largest(x_own), largest(protein_orbitals)])
    tops = jnp.broadcast_to(tops[:, None], (2, wide + LANES))
    tops = jnp.maximum(tops, other(tops, "c"))
    bound = (2.0 * mus) * tops[:1] * tops[1:]
    code = jnp.ceil(jnp.log2(jnp.maximum(bound, 1e-30))) + 1.0
    a_part = dot(orb_own, x_own, ((1,), (1,))) + dot(orb_other, x_other, ((1,), (1,)))
    a_sent = (a_part * jnp.exp2(15.0 - code[:, :wide])).astype(F16)
    code = jnp.broadcast_to(code[:, wide:].astype(F16), (n_zy * pro, LANES))
    a_sent = jnp.concatenate([a_sent, code], axis=1)
    a_got = exchange(a_sent.reshape(n_zy, pro, wide + LANES), ZY)
    codes = a_got[:, :1, wide : wide + 1].astype(F32)
    a_own = jnp.sum(a_got[:, :, :wide].astype(F32) * jnp.exp2(codes - 15.0), axis=0)

    b_blocks, b_places = direct_gather(b_own.astype(BF16), AA, aa)
    scale_ligand = 1.0 / math.sqrt(fit * pro_total)
    rows_b = nus // (2 * n_zy)
    keep, send = back_part(y, b_blocks, b_places, core, scale_ligand, rows_b)
    back_b = keep + other(send, "c")
    a_all = exchange(spread(back_b.reshape(-1, lig_total), a_own, n_zy), ZY).reshape(n_zy * pro, wide)
    back_b = pair_sum(back_b.reshape(n_z, n_yl, rows_b, lig_total), "yl")

    pair = jnp.sum(
        jnp.transpose(a_own.reshape(pro, fit, lig), (1, 2, 0))
        * jnp.transpose(b_own.reshape(lig, fit, pro), (1, 0, 2)),
        axis=0,
    )
    pair_exchange = -pair / math.sqrt(fit)

    scale_protein = 1.0 / math.sqrt(fit * lig_total)
    rows = mus // n_aa
    token = back_b.reshape(-1, lig_total)
    back_a = product(token, x_own, x_other, a_all, scale_protein, rows)
    ligand_back = direct_sum(back_b, ("z",), (n_z,), F32)
    back_a = exchange(back_a, AA)
    here, away = jnp.sum(back_a.astype(F32), axis=0)
    there = other(away, "c")
    here = here.reshape(rows, n_zy, 1, pro)
    there = there.reshape(rows, n_zy, 1, pro)
    protein_back = jnp.where(
        core == 0,
        jnp.concatenate([here, there], axis=2),
        jnp.concatenate([there, here], axis=2),
    ).reshape(rows, pro_total)
    return (pair_exchange, ligand_back, protein_back)


def solution(mesh):
    sizes = {"x": mesh.shape["aa"] // 2, "yh": 2, "z": mesh.shape["ba"] // 4, "yl": 2, "c": 2}
    fine = Mesh(mesh.devices.reshape([sizes[name] for name in AXES]), AXES)
    aa, ba = AA, ("z", "yl", "c")
    placed = (P(None, aa, ba), P(None, ba, aa), P(None, ba), P(None, aa))

    def body(*args):
        return on_device(*args, sizes=sizes)

    return jax.shard_map(
        body,
        mesh=fine,
        in_specs=placed,
        out_specs=(P(aa, ba), P(aa + ba, None), P(ba + aa, None)),
        check_vma=False,
    )
```

```python
import itertools
import math

import jax
import jax.numpy as jnp
from jax import lax
from jax.experimental import pallas as pl
from jax.experimental.pallas import tpu as pltpu
from jax.sharding import Mesh, PartitionSpec as P

AXES = ("x", "yh", "z", "yl", "c")
AA = ("x", "yh")
ZY = ("z", "yl")
F32 = jnp.float32
F16 = jnp.float16
BF16 = jnp.bfloat16
LANES = 128
VMEM = 16 * 2**20


def exchange(pieces, axes):
    return lax.all_to_all(pieces, axes, 0, 0, tiled=True)


def shifts(sizes):
    return list(itertools.product(*(range(size) for size in sizes)))[1:]


def flat(place, sizes):
    index = 0
    for part, size in zip(place, sizes):
        index = index * size + part
    return index


def moved(sizes, shift):
    places = itertools.product(*(range(size) for size in sizes))
    return [
        (flat(place, sizes), flat([(p + s) % n for p, s, n in zip(place, shift, sizes)], sizes))
        for place in places
    ]


def peer(axes, sizes, shift):
    return flat(
        [lax.rem(lax.axis_index(name) + s, n) for name, s, n in zip(axes, shift, sizes)], sizes
    )


def direct_sum(pieces, axes, sizes, sent):
    own = (0,) * len(sizes)
    total = lax.dynamic_index_in_dim(pieces, peer(axes, sizes, own), 0, keepdims=False).astype(F32)
    for shift in shifts(sizes):
        piece = lax.dynamic_index_in_dim(pieces, peer(axes, sizes, shift), 0, keepdims=False)
        total = total + lax.ppermute(piece.astype(sent), axes, moved(sizes, shift)).astype(F32)
    return total


def direct_gather(block, axes, sizes):
    blocks, places = [block], [peer(axes, sizes, (0,) * len(sizes))]
    for shift in shifts(sizes):
        blocks.append(lax.ppermute(block, axes, moved(sizes, shift)))
        places.append(peer(axes, sizes, [n - s for s, n in zip(shift, sizes)]))
    return blocks, places


def other(block, axis):
    return lax.ppermute(block, axis, [(0, 1), (1, 0)])


def pair_sum(pieces, axis):
    me = lax.axis_index(axis)
    keep = lax.dynamic_index_in_dim(pieces, me, 1, keepdims=False)
    send = lax.dynamic_index_in_dim(pieces, 1 - me, 1, keepdims=False)
    return keep + other(send, axis)


def in_order(mine, others, axis):
    first = lax.axis_index(axis) == 0
    return jnp.stack([jnp.where(first, mine, others), jnp.where(first, others, mine)])


def dot(left, right, contract):
    return lax.dot_general(left, right, (contract, ((), ())), preferred_element_type=F32)


def largest(array):
    return jnp.max(jnp.abs(array)).astype(F32)


def cross_kernel(token_ref, left_ref, right_ref, out_ref):
    del token_ref
    out_ref[...] = dot(left_ref[...], right_ref[...], ((1,), (1,))).astype(out_ref.dtype)


def cross_part(token, orbitals, slab):
    rows, depth = slab.shape
    step = min(rows, 256)
    return pl.pallas_call(
        cross_kernel,
        grid=(rows // step,),
        in_specs=[
            pl.BlockSpec(token.shape, lambda i: (0, 0)),
            pl.BlockSpec(orbitals.shape, lambda i: (0, 0)),
            pl.BlockSpec((step, depth), lambda i: (i, 0)),
        ],
        out_specs=pl.BlockSpec((orbitals.shape[0], step), lambda i: (0, i)),
        out_shape=jax.ShapeDtypeStruct((orbitals.shape[0], rows), BF16),
        compiler_params=pltpu.CompilerParams(vmem_limit_bytes=VMEM),
        cost_estimate=pl.CostEstimate(flops=0, bytes_accessed=0, transcendentals=0),
        name="cross_part",
    )(token, orbitals, slab)


def back_kernel(place_ref, slab_ref, *refs, count, scale, fine):
    blocks, (keep_ref, send_ref, all_ref) = refs[:count], refs[count:]

    @pl.when(pl.program_id(0) == 0)
    def _():
        for k, block_ref in enumerate(blocks):
            rows = block_ref.shape[0]
            all_ref[pl.ds(pl.multiple_of(place_ref[k] * rows, rows), rows), :] = block_ref[...]

    part = dot(all_ref[...], slab_ref[...], ((1,), (0,))) * scale
    part = part.T.reshape(-1, 2, fine, all_ref.shape[0])
    first, second = part[:, 0], part[:, 1]
    low = place_ref[count] == 0
    keep_ref[...] = jnp.where(low, first, second)
    send_ref[...] = jnp.where(low, second, first)


def back_part(slab, blocks, places, core, scale, fine):
    count = len(blocks)
    depth, total = slab.shape
    rows = blocks[0].shape[0]
    step = min(total, 256)
    out = pl.BlockSpec((step // (2 * fine), fine, count * rows), lambda i, _: (i, 0, 0))
    shape = jax.ShapeDtypeStruct((total // (2 * fine), fine, count * rows), F32)
    return pl.pallas_call(
        lambda *refs: back_kernel(*refs, count=count, scale=scale, fine=fine),
        grid_spec=pltpu.PrefetchScalarGridSpec(
            num_scalar_prefetch=1,
            grid=(total // step,),
            in_specs=[pl.BlockSpec((depth, step), lambda i, _: (0, i))]
            + [pl.BlockSpec((rows, depth), lambda i, _: (0, 0))] * count,
            out_specs=[out, out],
            scratch_shapes=[pltpu.VMEM((count * rows, depth), BF16)],
        ),
        out_shape=[shape, shape],
        compiler_params=pltpu.CompilerParams(vmem_limit_bytes=VMEM),
        cost_estimate=pl.CostEstimate(flops=0, bytes_accessed=0, transcendentals=0),
        name="back_part",
    )(jnp.stack(places + [core]).astype(jnp.int32), slab, *blocks)


def spread_kernel(*refs):
    block_ref, out_ref = refs[-2:]
    out_ref[...] = jnp.broadcast_to(block_ref[...].astype(out_ref.dtype)[None], out_ref.shape)


def spread(tokens, block, count):
    return pl.pallas_call(
        spread_kernel,
        grid=(1,),
        in_specs=[pl.BlockSpec((16, LANES), lambda i: (0, 0))] * len(tokens)
        + [pl.BlockSpec(block.shape, lambda i: (0, 0))],
        out_specs=pl.BlockSpec((count,) + block.shape, lambda i: (0, 0, 0)),
        out_shape=jax.ShapeDtypeStruct((count,) + block.shape, BF16),
        cost_estimate=pl.CostEstimate(flops=0, bytes_accessed=0, transcendentals=0),
        name="spread",
    )(*tokens, block)


def product_kernel(token_ref, own_ref, other_ref, right_ref, out_ref, *, scale, step):
    del token_ref
    runs = step // out_ref.shape[2]
    for i in range(own_ref.shape[1] // step):
        columns = pl.ds(i * step, step)
        for k, left_ref in enumerate((own_ref, other_ref)):
            part = dot(right_ref[...], left_ref[:, columns], ((1,), (0,))) * scale
            part = part.T.reshape(runs, out_ref.shape[2], right_ref.shape[0])
            out_ref[pl.ds(i * runs, runs), k] = part.astype(out_ref.dtype)


def product(token, own, other_core, right, scale, fine):
    total = own.shape[1]
    step = min(total, 256)
    whole = pl.BlockSpec(memory_space=pltpu.VMEM)
    return pl.pallas_call(
        lambda *refs: product_kernel(*refs, scale=scale, step=step),
        grid=(1,),
        in_specs=[pl.BlockSpec((8, LANES), lambda i: (0, 0)), whole, whole, whole],
        out_specs=whole,
        out_shape=jax.ShapeDtypeStruct((total // fine, 2, fine, right.shape[0]), BF16),
        compiler_params=pltpu.CompilerParams(vmem_limit_bytes=VMEM),
        cost_estimate=pl.CostEstimate(flops=0, bytes_accessed=0, transcendentals=0),
        name="product",
    )(token, own, other_core, right)


def on_device(ligand_slab, protein_slab, protein_orbitals, ligand_orbitals, *, sizes):
    aa = (sizes["x"], sizes["yh"])
    n_aa = aa[0] * aa[1]
    n_z, n_yl = sizes["z"], sizes["yl"]
    n_zy = n_z * n_yl
    fit, lig, mus = ligand_slab.shape
    _, pro, nus = protein_slab.shape
    lig_total, pro_total = ligand_orbitals.shape[0], protein_orbitals.shape[0]
    core = lax.axis_index("c")
    wide = fit * lig

    x_own = ligand_slab.reshape(wide, mus)
    y = protein_slab.reshape(fit * pro, nus)
    x_other = other(x_own, "c")
    orb = protein_orbitals.reshape(n_zy, 2, pro, mus)
    orb_own = lax.dynamic_index_in_dim(orb, core, 1, keepdims=False).reshape(n_zy * pro, mus)
    orb_send = lax.dynamic_index_in_dim(orb, 1 - core, 1, keepdims=False).reshape(n_zy * pro, mus)
    orb_other = other(orb_send, "c")

    tops = jnp.stack([largest(x_own), largest(protein_orbitals)])
    tops = jnp.broadcast_to(tops[:, None], (2, wide + LANES))
    tops = jnp.maximum(tops, other(tops, "c"))
    bound = (2.0 * mus) * tops[:1] * tops[1:]
    code = jnp.ceil(jnp.log2(jnp.maximum(bound, 1e-30))) + 1.0
    a_part = dot(orb_own, x_own, ((1,), (1,))) + dot(orb_other, x_other, ((1,), (1,)))
    a_sent = (a_part * jnp.exp2(15.0 - code[:, :wide])).astype(F16)
    code = jnp.broadcast_to(code[:, wide:].astype(F16), (n_zy * pro, LANES))
    a_sent = jnp.concatenate([a_sent, code], axis=1)
    a_got = exchange(a_sent.reshape(n_zy, pro, wide + LANES), ZY)
    codes = a_got[:, :1, wide : wide + 1].astype(F32)
    a_own = jnp.sum(a_got[:, :, :wide].astype(F32) * jnp.exp2(codes - 15.0), axis=0)

    b_part = cross_part(a_sent[:8, :LANES].astype(F32), ligand_orbitals, y)
    n_x, n_yh = aa
    b_own = direct_sum(b_part.reshape(n_x, n_yh * lig, fit * pro), ("x",), (n_x,), BF16)
    b_own = pair_sum(b_own.reshape(1, n_yh, lig, fit * pro), "yh").reshape(lig, fit * pro)
    b_pair = b_own.astype(BF16)
    b_pair = in_order(b_pair, other(b_pair, "yh"), "yh").reshape(n_yh * lig, fit * pro)
    b_blocks, b_places = direct_gather(b_pair, ("x",), (n_x,))
    a_all = exchange(spread(b_blocks[1:], a_own, n_zy), ZY).reshape(n_zy * pro, wide)

    pair = jnp.sum(
        jnp.transpose(a_own.reshape(pro, fit, lig), (1, 2, 0))
        * jnp.transpose(b_own.reshape(lig, fit, pro), (1, 0, 2)),
        axis=0,
    )
    pair_exchange = -pair / math.sqrt(fit)

    scale_ligand = 1.0 / math.sqrt(fit * pro_total)
    rows_b = nus // (2 * n_zy)
    keep, send = back_part(y, b_blocks, b_places, core, scale_ligand, rows_b)
    back_b = keep + other(send, "c")
    back_b = pair_sum(back_b.reshape(n_z, n_yl, rows_b, lig_total), "yl")
    ligand_back = direct_sum(back_b, ("z",), (n_z,), F32)

    scale_protein = 1.0 / math.sqrt(fit * lig_total)
    rows = mus // n_aa
    token = back_b.reshape(n_z * rows_b, lig_total)
    back_a = product(token, x_own, x_other, a_all, scale_protein, rows)
    back_a = exchange(back_a, AA)
    here, away = jnp.sum(back_a.astype(F32), axis=0)
    there = other(away, "c")
    here = here.reshape(rows, n_zy, 1, pro)
    there = there.reshape(rows, n_zy, 1, pro)
    protein_back = jnp.where(
        core == 0,
        jnp.concatenate([here, there], axis=2),
        jnp.concatenate([there, here], axis=2),
    ).reshape(rows, pro_total)
    return (pair_exchange, ligand_back, protein_back)


def solution(mesh):
    sizes = {"x": mesh.shape["aa"] // 2, "yh": 2, "z": mesh.shape["ba"] // 4, "yl": 2, "c": 2}
    fine = Mesh(mesh.devices.reshape([sizes[name] for name in AXES]), AXES)
    aa, ba = AA, ("z", "yl", "c")
    placed = (P(None, aa, ba), P(None, ba, aa), P(None, ba), P(None, aa))

    def body(*args):
        return on_device(*args, sizes=sizes)

    return jax.shard_map(
        body,
        mesh=fine,
        in_specs=placed,
        out_specs=(P(aa, ba), P(aa + ba, None), P(ba + aa, None)),
        check_vma=False,
    )
```

```python
import itertools
import math

import jax
import jax.numpy as jnp
from jax import lax
from jax.experimental import pallas as pl
from jax.experimental.pallas import tpu as pltpu
from jax.sharding import Mesh, PartitionSpec as P

AXES = ("x", "yh", "z", "yl", "c")
AA = ("x", "yh")
ZY = ("z", "yl")
F32 = jnp.float32
F16 = jnp.float16
BF16 = jnp.bfloat16
LANES = 128
VMEM = 16 * 2**20


def exchange(pieces, axes):
    return lax.all_to_all(pieces, axes, 0, 0, tiled=True)


def shifts(sizes):
    return list(itertools.product(*(range(size) for size in sizes)))[1:]


def flat(place, sizes):
    index = 0
    for part, size in zip(place, sizes):
        index = index * size + part
    return index


def moved(sizes, shift):
    places = itertools.product(*(range(size) for size in sizes))
    return [
        (flat(place, sizes), flat([(p + s) % n for p, s, n in zip(place, shift, sizes)], sizes))
        for place in places
    ]


def peer(axes, sizes, shift):
    return flat(
        [lax.rem(lax.axis_index(name) + s, n) for name, s, n in zip(axes, shift, sizes)], sizes
    )


def other(block, axis):
    return lax.ppermute(block, axis, [(0, 1), (1, 0)])


def pair_sum(pieces, axis):
    me = lax.axis_index(axis)
    keep = lax.dynamic_index_in_dim(pieces, me, 1, keepdims=False)
    send = lax.dynamic_index_in_dim(pieces, 1 - me, 1, keepdims=False)
    return keep + other(send, axis)


def in_order(mine, others, axis):
    first = lax.axis_index(axis) == 0
    return jnp.stack([jnp.where(first, mine, others), jnp.where(first, others, mine)])


def halves(sizes):
    every = [(0,) * len(sizes)] + shifts(sizes)
    half = len(every) // 2
    return every[1:half] + every[:1], every[half:]


def joint(block, axes, sizes, first, second):
    pairs = []
    for core, shift in enumerate((first, second)):
        if any(shift):
            pairs += [(2 * i + core, 2 * j + core) for i, j in moved(sizes, shift)]
    return lax.ppermute(block, axes + ("c",), pairs)


def shared(pieces, axes, sizes):
    first, second = (
        jnp.stack(
            [lax.dynamic_index_in_dim(pieces, peer(axes, sizes, shift), 0, keepdims=False) for shift in part]
        )
        for part in halves(sizes)
    )
    low = lax.axis_index("c") == 0
    return jnp.where(low, first, second), jnp.where(low, second, first)


def joint_sum(pieces, axes, sizes):
    keep, send = shared(pieces, axes, sizes)
    got = other(send, "c")
    total = 0.0
    for j, (first, second) in enumerate(zip(*halves(sizes))):
        block = in_order(keep[j], got[j], "c")
        total = total + joint(block, axes, sizes, first, second).astype(F32)
    own = lax.dynamic_index_in_dim(pieces, peer(axes, sizes, (0,) * len(sizes)), 0, keepdims=False)
    low = lax.axis_index("c") == 0
    mine, away = jnp.where(low, total[0], total[1]), jnp.where(low, total[1], total[0])
    return own.astype(F32) + (mine + other(away, "c"))


def joint_gather(block, axes, sizes):
    both = in_order(block, other(block, "c"), "c")
    low = lax.axis_index("c") == 0
    mine, away, mine_places, away_places = [], [], [], []
    for first, second in zip(*halves(sizes)):
        got = joint(both, axes, sizes, first, second)
        mine.append(jnp.where(low, got[0], got[1]))
        away.append(jnp.where(low, got[1], got[0]))
        one, two = (peer(axes, sizes, [n - p for p, n in zip(shift, sizes)]) for shift in (first, second))
        mine_places.append(jnp.where(low, one, two))
        away_places.append(jnp.where(low, two, one))
    theirs = other(jnp.stack(away), "c")
    blocks = mine + [theirs[j] for j in range(len(mine))] + [block]
    return blocks, mine_places + away_places + [peer(axes, sizes, (0,) * len(sizes))]


def dot(left, right, contract):
    return lax.dot_general(left, right, (contract, ((), ())), preferred_element_type=F32)


def largest(array):
    return jnp.max(jnp.abs(array)).astype(F32)


def cross_kernel(token_ref, left_ref, right_ref, out_ref):
    del token_ref
    out_ref[...] = dot(left_ref[...], right_ref[...], ((1,), (1,))).astype(out_ref.dtype)


def cross_part(token, orbitals, slab):
    rows, depth = slab.shape
    step = min(rows, 256)
    return pl.pallas_call(
        cross_kernel,
        grid=(rows // step,),
        in_specs=[
            pl.BlockSpec(token.shape, lambda i: (0, 0)),
            pl.BlockSpec(orbitals.shape, lambda i: (0, 0)),
            pl.BlockSpec((step, depth), lambda i: (i, 0)),
        ],
        out_specs=pl.BlockSpec((orbitals.shape[0], step), lambda i: (0, i)),
        out_shape=jax.ShapeDtypeStruct((orbitals.shape[0], rows), BF16),
        compiler_params=pltpu.CompilerParams(vmem_limit_bytes=VMEM),
        cost_estimate=pl.CostEstimate(flops=0, bytes_accessed=0, transcendentals=0),
        name="cross_part",
    )(token, orbitals, slab)


def back_kernel(place_ref, slab_ref, *refs, count, scale):
    blocks, (out_ref, all_ref) = refs[:count], refs[count:]

    @pl.when(pl.program_id(0) == 0)
    def _():
        for k, block_ref in enumerate(blocks):
            rows = block_ref.shape[0]
            all_ref[pl.ds(pl.multiple_of(place_ref[k] * rows, rows), rows), :] = block_ref[...]

    out_ref[...] = (dot(all_ref[...], slab_ref[...], ((1,), (0,))) * scale).T


def back_part(slab, blocks, places, scale, wide):
    count = len(blocks)
    depth, total = slab.shape
    step = min(total, 256)
    return pl.pallas_call(
        lambda *refs: back_kernel(*refs, count=count, scale=scale),
        grid_spec=pltpu.PrefetchScalarGridSpec(
            num_scalar_prefetch=1,
            grid=(total // step,),
            in_specs=[pl.BlockSpec((depth, step), lambda i, _: (0, i))]
            + [pl.BlockSpec(block.shape, lambda i, _: (0, 0)) for block in blocks],
            out_specs=pl.BlockSpec((step, wide), lambda i, _: (i, 0)),
            scratch_shapes=[pltpu.VMEM((wide, depth), BF16)],
        ),
        out_shape=jax.ShapeDtypeStruct((total, wide), F32),
        compiler_params=pltpu.CompilerParams(vmem_limit_bytes=VMEM),
        cost_estimate=pl.CostEstimate(flops=0, bytes_accessed=0, transcendentals=0),
        name="back_part",
    )(jnp.stack(places).astype(jnp.int32), slab, *blocks)


def spread_kernel(*refs):
    block_ref, out_ref = refs[-2:]
    out_ref[...] = jnp.broadcast_to(block_ref[...].astype(out_ref.dtype)[None], out_ref.shape)


def spread(tokens, block, count):
    return pl.pallas_call(
        spread_kernel,
        grid=(1,),
        in_specs=[pl.BlockSpec((16, LANES), lambda i: (0, 0))] * len(tokens)
        + [pl.BlockSpec(block.shape, lambda i: (0, 0))],
        out_specs=pl.BlockSpec((count,) + block.shape, lambda i: (0, 0, 0)),
        out_shape=jax.ShapeDtypeStruct((count,) + block.shape, BF16),
        cost_estimate=pl.CostEstimate(flops=0, bytes_accessed=0, transcendentals=0),
        name="spread",
    )(*tokens, block)


def product_kernel(token_ref, own_ref, other_ref, right_ref, out_ref, *, scale, step):
    del token_ref
    runs = step // out_ref.shape[2]
    for i in range(own_ref.shape[1] // step):
        columns = pl.ds(i * step, step)
        for k, left_ref in enumerate((own_ref, other_ref)):
            part = dot(right_ref[...], left_ref[:, columns], ((1,), (0,))) * scale
            part = part.T.reshape(runs, out_ref.shape[2], right_ref.shape[0])
            out_ref[pl.ds(i * runs, runs), k] = part.astype(out_ref.dtype)


def product(token, own, other_core, right, scale, fine):
    total = own.shape[1]
    step = min(total, 256)
    whole = pl.BlockSpec(memory_space=pltpu.VMEM)
    return pl.pallas_call(
        lambda *refs: product_kernel(*refs, scale=scale, step=step),
        grid=(1,),
        in_specs=[pl.BlockSpec((8, LANES), lambda i: (0, 0)), whole, whole, whole],
        out_specs=whole,
        out_shape=jax.ShapeDtypeStruct((total // fine, 2, fine, right.shape[0]), BF16),
        compiler_params=pltpu.CompilerParams(vmem_limit_bytes=VMEM),
        cost_estimate=pl.CostEstimate(flops=0, bytes_accessed=0, transcendentals=0),
        name="product",
    )(token, own, other_core, right)


def on_device(ligand_slab, protein_slab, protein_orbitals, ligand_orbitals, *, sizes):
    aa = (sizes["x"], sizes["yh"])
    n_aa = aa[0] * aa[1]
    n_z, n_yl = sizes["z"], sizes["yl"]
    n_zy = n_z * n_yl
    fit, lig, mus = ligand_slab.shape
    _, pro, nus = protein_slab.shape
    lig_total, pro_total = ligand_orbitals.shape[0], protein_orbitals.shape[0]
    core = lax.axis_index("c")
    wide = fit * lig

    x_own = ligand_slab.reshape(wide, mus)
    y = protein_slab.reshape(fit * pro, nus)
    x_other = other(x_own, "c")
    orb = protein_orbitals.reshape(n_zy, 2, pro, mus)
    orb_own = lax.dynamic_index_in_dim(orb, core, 1, keepdims=False).reshape(n_zy * pro, mus)
    orb_send = lax.dynamic_index_in_dim(orb, 1 - core, 1, keepdims=False).reshape(n_zy * pro, mus)
    orb_other = other(orb_send, "c")

    tops = jnp.stack([largest(x_own), largest(protein_orbitals)])
    tops = jnp.broadcast_to(tops[:, None], (2, wide + LANES))
    tops = jnp.maximum(tops, other(tops, "c"))
    bound = (2.0 * mus) * tops[:1] * tops[1:]
    code = jnp.ceil(jnp.log2(jnp.maximum(bound, 1e-30))) + 1.0
    a_part = dot(orb_own, x_own, ((1,), (1,))) + dot(orb_other, x_other, ((1,), (1,)))
    a_sent = (a_part * jnp.exp2(15.0 - code[:, :wide])).astype(F16)
    code = jnp.broadcast_to(code[:, wide:].astype(F16), (n_zy * pro, LANES))
    a_sent = jnp.concatenate([a_sent, code], axis=1)
    a_got = exchange(a_sent.reshape(n_zy, pro, wide + LANES), ZY)
    codes = a_got[:, :1, wide : wide + 1].astype(F32)
    a_own = jnp.sum(a_got[:, :, :wide].astype(F32) * jnp.exp2(codes - 15.0), axis=0)

    b_part = cross_part(a_sent[:8, :LANES].astype(F32), ligand_orbitals, y)
    b_own = joint_sum(b_part.reshape(n_aa, lig, fit * pro), AA, aa)
    a_all = exchange(spread([b_own], a_own, n_zy), ZY).reshape(n_zy * pro, wide)
    b_blocks, b_places = joint_gather(b_own.astype(BF16), AA, aa)

    pair = jnp.sum(
        jnp.transpose(a_own.reshape(pro, fit, lig), (1, 2, 0))
        * jnp.transpose(b_own.reshape(lig, fit, pro), (1, 0, 2)),
        axis=0,
    )
    pair_exchange = -pair / math.sqrt(fit)

    scale_ligand = 1.0 / math.sqrt(fit * pro_total)
    rows_b = nus // (2 * n_zy)
    back_b = back_part(y, b_blocks, b_places, scale_ligand, lig_total)
    keep, send = shared(back_b.reshape(n_z, nus // n_z, lig_total), ("z",), (n_z,))
    back_b = keep + other(send, "c")
    total = jnp.where(core == 0, back_b[-1], 0.0)
    for j, (first, second) in enumerate(zip(*halves((n_z,)))):
        total = total + joint(back_b[j].astype(BF16), ("z",), (n_z,), first, second).astype(F32)
    total = pair_sum(total.reshape(n_yl, 2, rows_b, lig_total), "c")
    ligand_back = pair_sum(total.reshape(1, n_yl, rows_b, lig_total), "yl").reshape(rows_b, lig_total)

    scale_protein = 1.0 / math.sqrt(fit * lig_total)
    rows = mus // n_aa
    token = back_b.reshape(-1, lig_total)
    back_a = product(token, x_own, x_other, a_all, scale_protein, rows)
    back_a = exchange(back_a, AA)
    here, away = jnp.sum(back_a.astype(F32), axis=0)
    there = other(away, "c")
    here = here.reshape(rows, n_zy, 1, pro)
    there = there.reshape(rows, n_zy, 1, pro)
    protein_back = jnp.where(
        core == 0,
        jnp.concatenate([here, there], axis=2),
        jnp.concatenate([there, here], axis=2),
    ).reshape(rows, pro_total)
    return (pair_exchange, ligand_back, protein_back)


def solution(mesh):
    sizes = {"x": mesh.shape["aa"] // 2, "yh": 2, "z": mesh.shape["ba"] // 4, "yl": 2, "c": 2}
    fine = Mesh(mesh.devices.reshape([sizes[name] for name in AXES]), AXES)
    aa, ba = AA, ("z", "yl", "c")
    placed = (P(None, aa, ba), P(None, ba, aa), P(None, ba), P(None, aa))

    def body(*args):
        return on_device(*args, sizes=sizes)

    return jax.shard_map(
        body,
        mesh=fine,
        in_specs=placed,
        out_specs=(P(aa, ba), P(aa + ba, None), P(ba + aa, None)),
        check_vma=False,
    )
```

```python
import itertools
import math

import jax
import jax.numpy as jnp
from jax import lax
from jax.experimental import pallas as pl
from jax.experimental.pallas import tpu as pltpu
from jax.sharding import Mesh, PartitionSpec as P

AXES = ("x", "yh", "z", "yl", "c")
AA = ("x", "yh")
ZY = ("z", "yl")
F32 = jnp.float32
F16 = jnp.float16
BF16 = jnp.bfloat16
LANES = 128
VMEM = 16 * 2**20


def exchange(pieces, axes):
    return lax.all_to_all(pieces, axes, 0, 0, tiled=True)


def shifts(sizes):
    return list(itertools.product(*(range(size) for size in sizes)))[1:]


def flat(place, sizes):
    index = 0
    for part, size in zip(place, sizes):
        index = index * size + part
    return index


def moved(sizes, shift):
    places = itertools.product(*(range(size) for size in sizes))
    return [
        (flat(place, sizes), flat([(p + s) % n for p, s, n in zip(place, shift, sizes)], sizes))
        for place in places
    ]


def peer(axes, sizes, shift):
    return flat(
        [lax.rem(lax.axis_index(name) + s, n) for name, s, n in zip(axes, shift, sizes)], sizes
    )


def other(block, axis):
    return lax.ppermute(block, axis, [(0, 1), (1, 0)])


def pair_sum(pieces, axis):
    me = lax.axis_index(axis)
    keep = lax.dynamic_index_in_dim(pieces, me, 1, keepdims=False)
    send = lax.dynamic_index_in_dim(pieces, 1 - me, 1, keepdims=False)
    return keep + other(send, axis)


def in_order(mine, others, axis):
    first = lax.axis_index(axis) == 0
    return jnp.stack([jnp.where(first, mine, others), jnp.where(first, others, mine)])


def halves(sizes):
    every = [(0,) * len(sizes)] + shifts(sizes)
    half = len(every) // 2
    return every[1:half] + every[:1], every[half:]


def joint(block, axes, sizes, first, second):
    pairs = []
    for core, shift in enumerate((first, second)):
        if any(shift):
            pairs += [(2 * i + core, 2 * j + core) for i, j in moved(sizes, shift)]
    return lax.ppermute(block, axes + ("c",), pairs)


def shared(pieces, axes, sizes):
    first, second = (
        jnp.stack(
            [lax.dynamic_index_in_dim(pieces, peer(axes, sizes, shift), 0, keepdims=False) for shift in part]
        )
        for part in halves(sizes)
    )
    low = lax.axis_index("c") == 0
    return jnp.where(low, first, second), jnp.where(low, second, first)


def joint_sum(pieces, axes, sizes):
    keep, send = shared(pieces, axes, sizes)
    got = other(send, "c")
    total = 0.0
    for j, (first, second) in enumerate(zip(*halves(sizes))):
        block = in_order(keep[j], got[j], "c")
        total = total + joint(block, axes, sizes, first, second).astype(F32)
    own = lax.dynamic_index_in_dim(pieces, peer(axes, sizes, (0,) * len(sizes)), 0, keepdims=False)
    low = lax.axis_index("c") == 0
    mine, away = jnp.where(low, total[0], total[1]), jnp.where(low, total[1], total[0])
    return own.astype(F32) + (mine + other(away, "c"))


def joint_gather(both, axes, sizes):
    low = lax.axis_index("c") == 0
    mine, away, mine_places, away_places = [], [], [], []
    for first, second in zip(*halves(sizes)):
        got = joint(both, axes, sizes, first, second)
        mine.append(jnp.where(low, got[0], got[1]))
        away.append(jnp.where(low, got[1], got[0]))
        one, two = (peer(axes, sizes, [n - p for p, n in zip(shift, sizes)]) for shift in (first, second))
        mine_places.append(jnp.where(low, one, two))
        away_places.append(jnp.where(low, two, one))
    theirs = other(jnp.stack(away), "c")
    blocks = mine + [theirs[j] for j in range(len(mine))] + [jnp.where(low, both[0], both[1])]
    return blocks, mine_places + away_places + [peer(axes, sizes, (0,) * len(sizes))]


def dot(left, right, contract):
    return lax.dot_general(left, right, (contract, ((), ())), preferred_element_type=F32)


def largest(array):
    return jnp.max(jnp.abs(array)).astype(F32)


def cross_kernel(token_ref, left_ref, right_ref, out_ref):
    del token_ref
    out_ref[...] = dot(left_ref[...], right_ref[...], ((1,), (1,))).astype(out_ref.dtype)


def cross_part(token, orbitals, slab):
    rows, depth = slab.shape
    step = min(rows, 256)
    return pl.pallas_call(
        cross_kernel,
        grid=(rows // step,),
        in_specs=[
            pl.BlockSpec(token.shape, lambda i: (0, 0)),
            pl.BlockSpec(orbitals.shape, lambda i: (0, 0)),
            pl.BlockSpec((step, depth), lambda i: (i, 0)),
        ],
        out_specs=pl.BlockSpec((orbitals.shape[0], step), lambda i: (0, i)),
        out_shape=jax.ShapeDtypeStruct((orbitals.shape[0], rows), BF16),
        compiler_params=pltpu.CompilerParams(vmem_limit_bytes=VMEM),
        cost_estimate=pl.CostEstimate(flops=0, bytes_accessed=0, transcendentals=0),
        name="cross_part",
    )(token, orbitals, slab)


def back_kernel(place_ref, slab_ref, *refs, count, scale):
    blocks, (out_ref, all_ref) = refs[:count], refs[count:]

    @pl.when(pl.program_id(0) == 0)
    def _():
        for k, block_ref in enumerate(blocks):
            rows = block_ref.shape[0]
            all_ref[pl.ds(pl.multiple_of(place_ref[k] * rows, rows), rows), :] = block_ref[...]

    out_ref[...] = (dot(all_ref[...], slab_ref[...], ((1,), (0,))) * scale).T


def back_part(slab, blocks, places, scale, wide):
    count = len(blocks)
    depth, total = slab.shape
    step = min(total, 256)
    return pl.pallas_call(
        lambda *refs: back_kernel(*refs, count=count, scale=scale),
        grid_spec=pltpu.PrefetchScalarGridSpec(
            num_scalar_prefetch=1,
            grid=(total // step,),
            in_specs=[pl.BlockSpec((depth, step), lambda i, _: (0, i))]
            + [pl.BlockSpec(block.shape, lambda i, _: (0, 0)) for block in blocks],
            out_specs=pl.BlockSpec((step, wide), lambda i, _: (i, 0)),
            scratch_shapes=[pltpu.VMEM((wide, depth), BF16)],
        ),
        out_shape=jax.ShapeDtypeStruct((total, wide), F32),
        compiler_params=pltpu.CompilerParams(vmem_limit_bytes=VMEM),
        cost_estimate=pl.CostEstimate(flops=0, bytes_accessed=0, transcendentals=0),
        name="back_part",
    )(jnp.stack(places).astype(jnp.int32), slab, *blocks)


def spread_kernel(pair_ref, block_ref, out_ref, copy_ref):
    out_ref[...] = jnp.broadcast_to(block_ref[...].astype(out_ref.dtype)[None], out_ref.shape)
    copy_ref[...] = pair_ref[...]


def spread(pair, block, count):
    whole = pl.BlockSpec(pair.shape, lambda i: (0, 0))
    return pl.pallas_call(
        spread_kernel,
        grid=(1,),
        in_specs=[whole, pl.BlockSpec(block.shape, lambda i: (0, 0))],
        out_specs=[pl.BlockSpec((count,) + block.shape, lambda i: (0, 0, 0)), whole],
        out_shape=[
            jax.ShapeDtypeStruct((count,) + block.shape, BF16),
            jax.ShapeDtypeStruct(pair.shape, pair.dtype),
        ],
        cost_estimate=pl.CostEstimate(flops=0, bytes_accessed=0, transcendentals=0),
        name="spread",
    )(pair, block)


def product_kernel(parts_ref, own_ref, other_ref, right_ref, out_ref, sent_ref, *, scale, step):
    runs = step // out_ref.shape[2]
    for i in range(own_ref.shape[1] // step):
        columns = pl.ds(i * step, step)
        for k, left_ref in enumerate((own_ref, other_ref)):
            part = dot(right_ref[...], left_ref[:, columns], ((1,), (0,))) * scale
            part = part.T.reshape(runs, out_ref.shape[2], right_ref.shape[0])
            out_ref[pl.ds(i * runs, runs), k] = part.astype(out_ref.dtype)
    sent_ref[...] = parts_ref[...].astype(sent_ref.dtype)


def product(parts, own, other_core, right, scale, fine):
    total = own.shape[1]
    step = min(total, 256)
    whole = pl.BlockSpec(memory_space=pltpu.VMEM)
    return pl.pallas_call(
        lambda *refs: product_kernel(*refs, scale=scale, step=step),
        in_specs=[whole] * 4,
        out_specs=[whole] * 2,
        out_shape=[
            jax.ShapeDtypeStruct((total // fine, 2, fine, right.shape[0]), BF16),
            jax.ShapeDtypeStruct(parts.shape, BF16),
        ],
        compiler_params=pltpu.CompilerParams(vmem_limit_bytes=VMEM),
        cost_estimate=pl.CostEstimate(flops=0, bytes_accessed=0, transcendentals=0),
        name="product",
    )(parts, own, other_core, right)


def on_device(ligand_slab, protein_slab, protein_orbitals, ligand_orbitals, *, sizes):
    aa = (sizes["x"], sizes["yh"])
    n_aa = aa[0] * aa[1]
    n_z, n_yl = sizes["z"], sizes["yl"]
    n_zy = n_z * n_yl
    fit, lig, mus = ligand_slab.shape
    _, pro, nus = protein_slab.shape
    lig_total, pro_total = ligand_orbitals.shape[0], protein_orbitals.shape[0]
    core = lax.axis_index("c")
    wide = fit * lig

    x_own = ligand_slab.reshape(wide, mus)
    y = protein_slab.reshape(fit * pro, nus)
    x_other = other(x_own, "c")
    orb = protein_orbitals.reshape(n_zy, 2, pro, mus)
    orb_own = lax.dynamic_index_in_dim(orb, core, 1, keepdims=False).reshape(n_zy * pro, mus)
    orb_send = lax.dynamic_index_in_dim(orb, 1 - core, 1, keepdims=False).reshape(n_zy * pro, mus)
    orb_other = other(orb_send, "c")

    tops = jnp.stack([largest(x_own), largest(protein_orbitals)])
    tops = jnp.broadcast_to(tops[:, None], (2, wide + LANES))
    tops = jnp.maximum(tops, other(tops, "c"))
    bound = (2.0 * mus) * tops[:1] * tops[1:]
    code = jnp.ceil(jnp.log2(jnp.maximum(bound, 1e-30))) + 1.0
    a_part = dot(orb_own, x_own, ((1,), (1,))) + dot(orb_other, x_other, ((1,), (1,)))
    a_sent = (a_part * jnp.exp2(15.0 - code[:, :wide])).astype(F16)
    code = jnp.broadcast_to(code[:, wide:].astype(F16), (n_zy * pro, LANES))
    a_sent = jnp.concatenate([a_sent, code], axis=1)
    a_got = exchange(a_sent.reshape(n_zy, pro, wide + LANES), ZY)
    codes = a_got[:, :1, wide : wide + 1].astype(F32)
    a_own = jnp.sum(a_got[:, :, :wide].astype(F32) * jnp.exp2(codes - 15.0), axis=0)

    b_part = cross_part(a_sent[:8, :LANES].astype(F32), ligand_orbitals, y)
    b_own = joint_sum(b_part.reshape(n_aa, lig, fit * pro), AA, aa)
    b_pair = b_own.astype(BF16)
    b_pair = in_order(b_pair, other(b_pair, "c"), "c").reshape(2 * lig, fit * pro)
    a_block, b_pair = spread(b_pair, a_own, n_zy)
    a_all = exchange(a_block, ZY).reshape(n_zy * pro, wide)
    b_blocks, b_places = joint_gather(b_pair.reshape(2, lig, fit * pro), AA, aa)

    pair = jnp.sum(
        jnp.transpose(a_own.reshape(pro, fit, lig), (1, 2, 0))
        * jnp.transpose(b_own.reshape(lig, fit, pro), (1, 0, 2)),
        axis=0,
    )
    pair_exchange = -pair / math.sqrt(fit)

    scale_ligand = 1.0 / math.sqrt(fit * pro_total)
    rows_b = nus // (2 * n_zy)
    back_b = back_part(y, b_blocks, b_places, scale_ligand, lig_total)
    keep, send = shared(back_b.reshape(n_z, nus // n_z, lig_total), ("z",), (n_z,))
    back_b = keep + other(send, "c")
    scale_protein = 1.0 / math.sqrt(fit * lig_total)
    rows = mus // n_aa
    back_a, sent = product(back_b, x_own, x_other, a_all, scale_protein, rows)

    total = jnp.where(core == 0, back_b[-1], 0.0)
    for j, (first, second) in enumerate(zip(*halves((n_z,)))):
        total = total + joint(sent[j], ("z",), (n_z,), first, second).astype(F32)
    total = pair_sum(total.reshape(n_yl, 2, rows_b, lig_total), "c")
    ligand_back = pair_sum(total.reshape(1, n_yl, rows_b, lig_total), "yl").reshape(rows_b, lig_total)

    back_a = exchange(back_a, AA)
    here, away = jnp.sum(back_a.astype(F32), axis=0)
    there = other(away, "c")
    here = here.reshape(rows, n_zy, 1, pro)
    there = there.reshape(rows, n_zy, 1, pro)
    protein_back = jnp.where(
        core == 0,
        jnp.concatenate([here, there], axis=2),
        jnp.concatenate([there, here], axis=2),
    ).reshape(rows, pro_total)
    return (pair_exchange, ligand_back, protein_back)


def solution(mesh):
    sizes = {"x": mesh.shape["aa"] // 2, "yh": 2, "z": mesh.shape["ba"] // 4, "yl": 2, "c": 2}
    fine = Mesh(mesh.devices.reshape([sizes[name] for name in AXES]), AXES)
    aa, ba = AA, ("z", "yl", "c")
    placed = (P(None, aa, ba), P(None, ba, aa), P(None, ba), P(None, aa))

    def body(*args):
        return on_device(*args, sizes=sizes)

    return jax.shard_map(
        body,
        mesh=fine,
        in_specs=placed,
        out_specs=(P(aa, ba), P(aa + ba, None), P(ba + aa, None)),
        check_vma=False,
    )
```

```python
import itertools
import math

import jax
import jax.numpy as jnp
from jax import lax
from jax.experimental import pallas as pl
from jax.experimental.pallas import tpu as pltpu
from jax.sharding import Mesh, PartitionSpec as P

AXES = ("x", "yh", "z", "yl", "c")
AA = ("x", "yh")
ZY = ("z", "yl")
F32 = jnp.float32
F16 = jnp.float16
BF16 = jnp.bfloat16
LANES = 128
VMEM = 16 * 2**20


def exchange(pieces, axes):
    return lax.all_to_all(pieces, axes, 0, 0, tiled=True)


def shifts(sizes):
    return list(itertools.product(*(range(size) for size in sizes)))[1:]


def flat(place, sizes):
    index = 0
    for part, size in zip(place, sizes):
        index = index * size + part
    return index


def moved(sizes, shift):
    places = itertools.product(*(range(size) for size in sizes))
    return [
        (flat(place, sizes), flat([(p + s) % n for p, s, n in zip(place, shift, sizes)], sizes))
        for place in places
    ]


def peer(axes, sizes, shift):
    return flat(
        [lax.rem(lax.axis_index(name) + s, n) for name, s, n in zip(axes, shift, sizes)], sizes
    )


def other(block, axis):
    return lax.ppermute(block, axis, [(0, 1), (1, 0)])


def pair_sum(pieces, axis):
    me = lax.axis_index(axis)
    keep = lax.dynamic_index_in_dim(pieces, me, 1, keepdims=False)
    send = lax.dynamic_index_in_dim(pieces, 1 - me, 1, keepdims=False)
    return keep + other(send, axis)


def in_order(mine, others, axis):
    first = lax.axis_index(axis) == 0
    return jnp.stack([jnp.where(first, mine, others), jnp.where(first, others, mine)])


def halves(sizes):
    every = [(0,) * len(sizes)] + shifts(sizes)
    half = len(every) // 2
    return every[1:half] + every[:1], every[half:]


def joint(block, axes, sizes, first, second):
    pairs = []
    for core, shift in enumerate((first, second)):
        if any(shift):
            pairs += [(2 * i + core, 2 * j + core) for i, j in moved(sizes, shift)]
    return lax.ppermute(block, axes + ("c",), pairs)


def shared(pieces, axes, sizes):
    first, second = (
        jnp.stack(
            [lax.dynamic_index_in_dim(pieces, peer(axes, sizes, shift), 0, keepdims=False) for shift in part]
        )
        for part in halves(sizes)
    )
    low = lax.axis_index("c") == 0
    return jnp.where(low, first, second), jnp.where(low, second, first)


def joint_sum(pieces, axes, sizes):
    keep, send = shared(pieces, axes, sizes)
    got = other(send, "c")
    total = 0.0
    for j, (first, second) in enumerate(zip(*halves(sizes))):
        block = in_order(keep[j], got[j], "c")
        total = total + joint(block, axes, sizes, first, second).astype(F32)
    own = lax.dynamic_index_in_dim(pieces, peer(axes, sizes, (0,) * len(sizes)), 0, keepdims=False)
    low = lax.axis_index("c") == 0
    mine, away = jnp.where(low, total[0], total[1]), jnp.where(low, total[1], total[0])
    return own.astype(F32) + (mine + other(away, "c"))


def joint_gather(both, axes, sizes):
    low = lax.axis_index("c") == 0
    mine, away, mine_places, away_places = [], [], [], []
    for first, second in zip(*halves(sizes)):
        got = joint(both, axes, sizes, first, second)
        mine.append(jnp.where(low, got[0], got[1]))
        away.append(jnp.where(low, got[1], got[0]))
        one, two = (peer(axes, sizes, [n - p for p, n in zip(shift, sizes)]) for shift in (first, second))
        mine_places.append(jnp.where(low, one, two))
        away_places.append(jnp.where(low, two, one))
    theirs = other(jnp.stack(away), "c")
    blocks = mine + [theirs[j] for j in range(len(mine))] + [jnp.where(low, both[0], both[1])]
    return blocks, mine_places + away_places + [peer(axes, sizes, (0,) * len(sizes))]


def dot(left, right, contract):
    return lax.dot_general(left, right, (contract, ((), ())), preferred_element_type=F32)


def largest(array):
    return jnp.max(jnp.abs(array)).astype(F32)


def cross_kernel(token_ref, left_ref, right_ref, out_ref):
    del token_ref
    out_ref[...] = dot(left_ref[...], right_ref[...], ((1,), (1,))).astype(out_ref.dtype)


def cross_part(token, orbitals, slab):
    rows, depth = slab.shape
    step = min(rows, 256)
    return pl.pallas_call(
        cross_kernel,
        grid=(rows // step,),
        in_specs=[
            pl.BlockSpec(token.shape, lambda i: (0, 0)),
            pl.BlockSpec(orbitals.shape, lambda i: (0, 0)),
            pl.BlockSpec((step, depth), lambda i: (i, 0)),
        ],
        out_specs=pl.BlockSpec((orbitals.shape[0], step), lambda i: (0, i)),
        out_shape=jax.ShapeDtypeStruct((orbitals.shape[0], rows), BF16),
        compiler_params=pltpu.CompilerParams(vmem_limit_bytes=VMEM),
        cost_estimate=pl.CostEstimate(flops=0, bytes_accessed=0, transcendentals=0),
        name="cross_part",
    )(token, orbitals, slab)


def back_kernel(place_ref, slab_ref, *refs, count, scale):
    blocks, (out_ref, all_ref) = refs[:count], refs[count:]

    @pl.when(pl.program_id(0) == 0)
    def _():
        for k, block_ref in enumerate(blocks):
            rows = block_ref.shape[0]
            all_ref[pl.ds(pl.multiple_of(place_ref[k] * rows, rows), rows), :] = block_ref[...]

    out_ref[...] = (dot(all_ref[...], slab_ref[...], ((1,), (0,))) * scale).T


def back_part(slab, blocks, places, scale, wide):
    count = len(blocks)
    depth, total = slab.shape
    step = min(total, 256)
    return pl.pallas_call(
        lambda *refs: back_kernel(*refs, count=count, scale=scale),
        grid_spec=pltpu.PrefetchScalarGridSpec(
            num_scalar_prefetch=1,
            grid=(total // step,),
            in_specs=[pl.BlockSpec((depth, step), lambda i, _: (0, i))]
            + [pl.BlockSpec(block.shape, lambda i, _: (0, 0)) for block in blocks],
            out_specs=pl.BlockSpec((step, wide), lambda i, _: (i, 0)),
            scratch_shapes=[pltpu.VMEM((wide, depth), BF16)],
        ),
        out_shape=jax.ShapeDtypeStruct((total, wide), F32),
        compiler_params=pltpu.CompilerParams(vmem_limit_bytes=VMEM),
        cost_estimate=pl.CostEstimate(flops=0, bytes_accessed=0, transcendentals=0),
        name="back_part",
    )(jnp.stack(places).astype(jnp.int32), slab, *blocks)


def together(work, core, *operands):
    shapes = jax.eval_shape(work, *operands)

    def none(*_):
        return jax.tree.map(lambda shape: jnp.zeros(shape.shape, shape.dtype), shapes)

    return lax.cond(core >= 0, work, none, *operands)


def spread_kernel(pair_ref, block_ref, out_ref, copy_ref):
    out_ref[...] = jnp.broadcast_to(block_ref[...].astype(out_ref.dtype)[None], out_ref.shape)
    copy_ref[...] = pair_ref[...]


def spread(pair, block, count):
    whole = pl.BlockSpec(pair.shape, lambda i: (0, 0))
    return pl.pallas_call(
        spread_kernel,
        grid=(1,),
        in_specs=[whole, pl.BlockSpec(block.shape, lambda i: (0, 0))],
        out_specs=[pl.BlockSpec((count,) + block.shape, lambda i: (0, 0, 0)), whole],
        out_shape=[
            jax.ShapeDtypeStruct((count,) + block.shape, BF16),
            jax.ShapeDtypeStruct(pair.shape, pair.dtype),
        ],
        cost_estimate=pl.CostEstimate(flops=0, bytes_accessed=0, transcendentals=0),
        name="spread",
    )(pair, block)


def product_kernel(parts_ref, own_ref, other_ref, right_ref, out_ref, sent_ref, *, scale, step):
    runs = step // out_ref.shape[2]
    for i in range(own_ref.shape[1] // step):
        columns = pl.ds(i * step, step)
        for k, left_ref in enumerate((own_ref, other_ref)):
            part = dot(right_ref[...], left_ref[:, columns], ((1,), (0,))) * scale
            part = part.T.reshape(runs, out_ref.shape[2], right_ref.shape[0])
            out_ref[pl.ds(i * runs, runs), k] = part.astype(out_ref.dtype)
    sent_ref[...] = parts_ref[...].astype(sent_ref.dtype)


def product(parts, own, other_core, right, scale, fine):
    total = own.shape[1]
    step = min(total, 256)
    whole = pl.BlockSpec(memory_space=pltpu.VMEM)
    return pl.pallas_call(
        lambda *refs: product_kernel(*refs, scale=scale, step=step),
        in_specs=[whole] * 4,
        out_specs=[whole] * 2,
        out_shape=[
            jax.ShapeDtypeStruct((total // fine, 2, fine, right.shape[0]), BF16),
            jax.ShapeDtypeStruct(parts.shape, BF16),
        ],
        compiler_params=pltpu.CompilerParams(vmem_limit_bytes=VMEM),
        cost_estimate=pl.CostEstimate(flops=0, bytes_accessed=0, transcendentals=0),
        name="product",
    )(parts, own, other_core, right)


def on_device(ligand_slab, protein_slab, protein_orbitals, ligand_orbitals, *, sizes):
    aa = (sizes["x"], sizes["yh"])
    n_aa = aa[0] * aa[1]
    n_z, n_yl = sizes["z"], sizes["yl"]
    n_zy = n_z * n_yl
    fit, lig, mus = ligand_slab.shape
    _, pro, nus = protein_slab.shape
    lig_total, pro_total = ligand_orbitals.shape[0], protein_orbitals.shape[0]
    core = lax.axis_index("c")
    wide = fit * lig

    x_own = ligand_slab.reshape(wide, mus)
    y = protein_slab.reshape(fit * pro, nus)
    x_other = other(x_own, "c")
    orb = protein_orbitals.reshape(n_zy, 2, pro, mus)
    orb_own = lax.dynamic_index_in_dim(orb, core, 1, keepdims=False).reshape(n_zy * pro, mus)
    orb_send = lax.dynamic_index_in_dim(orb, 1 - core, 1, keepdims=False).reshape(n_zy * pro, mus)
    orb_other = other(orb_send, "c")

    tops = jnp.stack([largest(x_own), largest(protein_orbitals)])
    tops = jnp.broadcast_to(tops[:, None], (2, wide + LANES))
    tops = jnp.maximum(tops, other(tops, "c"))
    bound = (2.0 * mus) * tops[:1] * tops[1:]
    code = jnp.ceil(jnp.log2(jnp.maximum(bound, 1e-30))) + 1.0
    a_part = dot(orb_own, x_own, ((1,), (1,))) + dot(orb_other, x_other, ((1,), (1,)))
    a_sent = (a_part * jnp.exp2(15.0 - code[:, :wide])).astype(F16)
    code = jnp.broadcast_to(code[:, wide:].astype(F16), (n_zy * pro, LANES))
    a_sent = jnp.concatenate([a_sent, code], axis=1)
    a_got = exchange(a_sent.reshape(n_zy, pro, wide + LANES), ZY)
    codes = a_got[:, :1, wide : wide + 1].astype(F32)
    a_own = jnp.sum(a_got[:, :, :wide].astype(F32) * jnp.exp2(codes - 15.0), axis=0)

    def sum_b(token, orbitals, slab):
        b_part = cross_part(token, orbitals, slab)
        b_own = joint_sum(b_part.reshape(n_aa, lig, fit * pro), AA, aa)
        b_pair = b_own.astype(BF16)
        return b_own, in_order(b_pair, other(b_pair, "c"), "c").reshape(2 * lig, fit * pro)

    b_own, b_pair = together(sum_b, core, a_sent[:8, :LANES].astype(F32), ligand_orbitals, y)
    a_block, b_pair = spread(b_pair, a_own, n_zy)
    a_all = exchange(a_block, ZY).reshape(n_zy * pro, wide)
    pair = jnp.sum(
        jnp.transpose(a_own.reshape(pro, fit, lig), (1, 2, 0))
        * jnp.transpose(b_own.reshape(lig, fit, pro), (1, 0, 2)),
        axis=0,
    )
    pair_exchange = -pair / math.sqrt(fit)

    scale_ligand = 1.0 / math.sqrt(fit * pro_total)
    rows_b = nus // (2 * n_zy)

    def multiply_b(b_pair, slab):
        blocks, places = joint_gather(b_pair.reshape(2, lig, fit * pro), AA, aa)
        back_b = back_part(slab, blocks, places, scale_ligand, lig_total)
        keep, send = shared(back_b.reshape(n_z, nus // n_z, lig_total), ("z",), (n_z,))
        return keep + other(send, "c")

    back_b = together(multiply_b, core, b_pair, y)

    scale_protein = 1.0 / math.sqrt(fit * lig_total)
    rows = mus // n_aa
    back_a, sent = product(back_b, x_own, x_other, a_all, scale_protein, rows)

    def sum_back(back_b, sent):
        total = jnp.where(core == 0, back_b[-1], 0.0)
        for j, (first, second) in enumerate(zip(*halves((n_z,)))):
            total = total + joint(sent[j], ("z",), (n_z,), first, second).astype(F32)
        total = pair_sum(total.reshape(n_yl, 2, rows_b, lig_total), "c")
        return pair_sum(total.reshape(1, n_yl, rows_b, lig_total), "yl").reshape(rows_b, lig_total)

    ligand_back = together(sum_back, core, back_b, sent)
    back_a = exchange(back_a, AA)
    here, away = jnp.sum(back_a.astype(F32), axis=0)
    there = other(away + 0.0 * ligand_back[:1, :1], "c")
    here = here.reshape(rows, n_zy, 1, pro)
    there = there.reshape(rows, n_zy, 1, pro)
    protein_back = jnp.where(
        core == 0,
        jnp.concatenate([here, there], axis=2),
        jnp.concatenate([there, here], axis=2),
    ).reshape(rows, pro_total)
    return (pair_exchange, ligand_back, protein_back)


def solution(mesh):
    sizes = {"x": mesh.shape["aa"] // 2, "yh": 2, "z": mesh.shape["ba"] // 4, "yl": 2, "c": 2}
    fine = Mesh(mesh.devices.reshape([sizes[name] for name in AXES]), AXES)
    aa, ba = AA, ("z", "yl", "c")
    placed = (P(None, aa, ba), P(None, ba, aa), P(None, ba), P(None, aa))

    def body(*args):
        return on_device(*args, sizes=sizes)

    return jax.shard_map(
        body,
        mesh=fine,
        in_specs=placed,
        out_specs=(P(aa, ba), P(aa + ba, None), P(ba + aa, None)),
        check_vma=False,
    )
```

```python
import itertools
import math

import jax
import jax.numpy as jnp
from jax import lax
from jax.experimental import pallas as pl
from jax.experimental.pallas import tpu as pltpu
from jax.sharding import Mesh, PartitionSpec as P

AXES = ("x", "yh", "z", "yl", "c")
AA = ("x", "yh")
ZY = ("z", "yl")
F32 = jnp.float32
F16 = jnp.float16
BF16 = jnp.bfloat16
LANES = 128
VMEM = 16 * 2**20


def exchange(pieces, axes):
    return lax.all_to_all(pieces, axes, 0, 0, tiled=True)


def shifts(sizes):
    return list(itertools.product(*(range(size) for size in sizes)))[1:]


def flat(place, sizes):
    index = 0
    for part, size in zip(place, sizes):
        index = index * size + part
    return index


def moved(sizes, shift):
    places = itertools.product(*(range(size) for size in sizes))
    return [
        (flat(place, sizes), flat([(p + s) % n for p, s, n in zip(place, shift, sizes)], sizes))
        for place in places
    ]


def peer(axes, sizes, shift):
    return flat(
        [lax.rem(lax.axis_index(name) + s, n) for name, s, n in zip(axes, shift, sizes)], sizes
    )


def other(block, axis):
    return lax.ppermute(block, axis, [(0, 1), (1, 0)])


def direct_sum(pieces, axes, sizes):
    own = (0,) * len(sizes)
    total = lax.dynamic_index_in_dim(pieces, peer(axes, sizes, own), 0, keepdims=False)
    for shift in shifts(sizes):
        piece = lax.dynamic_index_in_dim(pieces, peer(axes, sizes, shift), 0, keepdims=False)
        total = total + lax.ppermute(piece, axes, moved(sizes, shift))
    return total


def in_order(mine, others, axis):
    first = lax.axis_index(axis) == 0
    return jnp.stack([jnp.where(first, mine, others), jnp.where(first, others, mine)])


def halves(sizes):
    every = [(0,) * len(sizes)] + shifts(sizes)
    half = len(every) // 2
    return every[1:half] + every[:1], every[half:]


def joint(block, axes, sizes, first, second):
    pairs = []
    for core, shift in enumerate((first, second)):
        if any(shift):
            pairs += [(2 * i + core, 2 * j + core) for i, j in moved(sizes, shift)]
    return lax.ppermute(block, axes + ("c",), pairs)


def shared(pieces, axes, sizes):
    first, second = (
        jnp.stack(
            [lax.dynamic_index_in_dim(pieces, peer(axes, sizes, shift), 0, keepdims=False) for shift in part]
        )
        for part in halves(sizes)
    )
    low = lax.axis_index("c") == 0
    return jnp.where(low, first, second), jnp.where(low, second, first)


def joint_sum(pieces, axes, sizes):
    keep, send = shared(pieces, axes, sizes)
    got = other(send, "c")
    total = 0.0
    for j, (first, second) in enumerate(zip(*halves(sizes))):
        block = in_order(keep[j], got[j], "c")
        total = total + joint(block, axes, sizes, first, second).astype(F32)
    own = lax.dynamic_index_in_dim(pieces, peer(axes, sizes, (0,) * len(sizes)), 0, keepdims=False)
    low = lax.axis_index("c") == 0
    mine, away = jnp.where(low, total[0], total[1]), jnp.where(low, total[1], total[0])
    return own.astype(F32) + (mine + other(away, "c"))


def joint_gather(both, axes, sizes):
    low = lax.axis_index("c") == 0
    mine, away, mine_places, away_places = [], [], [], []
    for first, second in zip(*halves(sizes)):
        got = joint(both, axes, sizes, first, second)
        mine.append(jnp.where(low, got[0], got[1]))
        away.append(jnp.where(low, got[1], got[0]))
        one, two = (peer(axes, sizes, [n - p for p, n in zip(shift, sizes)]) for shift in (first, second))
        mine_places.append(jnp.where(low, one, two))
        away_places.append(jnp.where(low, two, one))
    theirs = other(jnp.stack(away), "c")
    blocks = mine + [theirs[j] for j in range(len(mine))] + [jnp.where(low, both[0], both[1])]
    return blocks, mine_places + away_places + [peer(axes, sizes, (0,) * len(sizes))]


def dot(left, right, contract):
    return lax.dot_general(left, right, (contract, ((), ())), preferred_element_type=F32)


def largest(array):
    return jnp.max(jnp.abs(array)).astype(F32)


def cross_kernel(token_ref, left_ref, right_ref, out_ref):
    del token_ref
    out_ref[...] = dot(left_ref[...], right_ref[...], ((1,), (1,))).astype(out_ref.dtype)


def cross_part(token, orbitals, slab):
    rows, depth = slab.shape
    step = min(rows, 256)
    return pl.pallas_call(
        cross_kernel,
        grid=(rows // step,),
        in_specs=[
            pl.BlockSpec(token.shape, lambda i: (0, 0)),
            pl.BlockSpec(orbitals.shape, lambda i: (0, 0)),
            pl.BlockSpec((step, depth), lambda i: (i, 0)),
        ],
        out_specs=pl.BlockSpec((orbitals.shape[0], step), lambda i: (0, i)),
        out_shape=jax.ShapeDtypeStruct((orbitals.shape[0], rows), BF16),
        compiler_params=pltpu.CompilerParams(vmem_limit_bytes=VMEM),
        cost_estimate=pl.CostEstimate(flops=0, bytes_accessed=0, transcendentals=0),
        name="cross_part",
    )(token, orbitals, slab)


def back_kernel(place_ref, slab_ref, *refs, count, scale):
    blocks, (out_ref, all_ref) = refs[:count], refs[count:]

    @pl.when(pl.program_id(0) == 0)
    def _():
        for k, block_ref in enumerate(blocks):
            rows = block_ref.shape[0]
            all_ref[pl.ds(pl.multiple_of(place_ref[k] * rows, rows), rows), :] = block_ref[...]

    out_ref[...] = (dot(all_ref[...], slab_ref[...], ((1,), (0,))) * scale).T


def back_part(slab, blocks, places, scale, wide):
    count = len(blocks)
    depth, total = slab.shape
    step = min(total, 256)
    return pl.pallas_call(
        lambda *refs: back_kernel(*refs, count=count, scale=scale),
        grid_spec=pltpu.PrefetchScalarGridSpec(
            num_scalar_prefetch=1,
            grid=(total // step,),
            in_specs=[pl.BlockSpec((depth, step), lambda i, _: (0, i))]
            + [pl.BlockSpec(block.shape, lambda i, _: (0, 0)) for block in blocks],
            out_specs=pl.BlockSpec((step, wide), lambda i, _: (i, 0)),
            scratch_shapes=[pltpu.VMEM((wide, depth), BF16)],
        ),
        out_shape=jax.ShapeDtypeStruct((total, wide), F32),
        compiler_params=pltpu.CompilerParams(vmem_limit_bytes=VMEM),
        cost_estimate=pl.CostEstimate(flops=0, bytes_accessed=0, transcendentals=0),
        name="back_part",
    )(jnp.stack(places).astype(jnp.int32), slab, *blocks)


def together(work, core, *operands):
    shapes = jax.eval_shape(work, *operands)

    def none(*_):
        return jax.tree.map(lambda shape: jnp.zeros(shape.shape, shape.dtype), shapes)

    return lax.cond(core >= 0, work, none, *operands)


def spread_kernel(pair_ref, block_ref, out_ref, copy_ref):
    out_ref[...] = jnp.broadcast_to(block_ref[...].astype(out_ref.dtype)[None], out_ref.shape)
    copy_ref[...] = pair_ref[...]


def spread(pair, block, count):
    whole = pl.BlockSpec(memory_space=pltpu.VMEM)
    return pl.pallas_call(
        spread_kernel,
        in_specs=[whole, whole],
        out_specs=[whole, whole],
        out_shape=[
            jax.ShapeDtypeStruct((count,) + block.shape, BF16),
            jax.ShapeDtypeStruct(pair.shape, pair.dtype),
        ],
        compiler_params=pltpu.CompilerParams(vmem_limit_bytes=VMEM),
        cost_estimate=pl.CostEstimate(flops=0, bytes_accessed=0, transcendentals=0),
        name="spread",
    )(pair, block)


def product_kernel(parts_ref, own_ref, other_ref, right_ref, out_ref, sent_ref, *, scale, step):
    runs = step // out_ref.shape[2]
    for i in range(own_ref.shape[1] // step):
        columns = pl.ds(i * step, step)
        for k, left_ref in enumerate((own_ref, other_ref)):
            part = dot(right_ref[...], left_ref[:, columns], ((1,), (0,))) * scale
            part = part.T.reshape(runs, out_ref.shape[2], right_ref.shape[0])
            out_ref[pl.ds(i * runs, runs), k] = part.astype(out_ref.dtype)
    sent_ref[...] = parts_ref[...].astype(sent_ref.dtype)


def product(parts, own, other_core, right, scale, fine):
    total = own.shape[1]
    step = min(total, 256)
    whole = pl.BlockSpec(memory_space=pltpu.VMEM)
    return pl.pallas_call(
        lambda *refs: product_kernel(*refs, scale=scale, step=step),
        in_specs=[whole] * 4,
        out_specs=[whole] * 2,
        out_shape=[
            jax.ShapeDtypeStruct((total // fine, 2, fine, right.shape[0]), BF16),
            jax.ShapeDtypeStruct(parts.shape, BF16),
        ],
        compiler_params=pltpu.CompilerParams(vmem_limit_bytes=VMEM),
        cost_estimate=pl.CostEstimate(flops=0, bytes_accessed=0, transcendentals=0),
        name="product",
    )(parts, own, other_core, right)


def on_device(ligand_slab, protein_slab, protein_orbitals, ligand_orbitals, *, sizes):
    aa = (sizes["x"], sizes["yh"])
    n_aa = aa[0] * aa[1]
    n_z, n_yl = sizes["z"], sizes["yl"]
    n_zy = n_z * n_yl
    fit, lig, mus = ligand_slab.shape
    _, pro, nus = protein_slab.shape
    lig_total, pro_total = ligand_orbitals.shape[0], protein_orbitals.shape[0]
    core = lax.axis_index("c")
    wide = fit * lig

    x_own = ligand_slab.reshape(wide, mus)
    y = protein_slab.reshape(fit * pro, nus)
    x_other = other(x_own, "c")
    orb = protein_orbitals.reshape(n_zy, 2, pro, mus)
    orb_own = lax.dynamic_index_in_dim(orb, core, 1, keepdims=False).reshape(n_zy * pro, mus)
    orb_send = lax.dynamic_index_in_dim(orb, 1 - core, 1, keepdims=False).reshape(n_zy * pro, mus)
    orb_other = other(orb_send, "c")

    tops = jnp.stack([largest(x_own), largest(protein_orbitals)])
    tops = jnp.broadcast_to(tops[:, None], (2, wide + LANES))
    tops = jnp.maximum(tops, other(tops, "c"))
    bound = (2.0 * mus) * tops[:1] * tops[1:]
    code = jnp.ceil(jnp.log2(jnp.maximum(bound, 1e-30))) + 1.0
    a_part = dot(orb_own, x_own, ((1,), (1,))) + dot(orb_other, x_other, ((1,), (1,)))
    a_sent = (a_part * jnp.exp2(15.0 - code[:, :wide])).astype(F16)
    code = jnp.broadcast_to(code[:, wide:].astype(F16), (n_zy * pro, LANES))
    a_sent = jnp.concatenate([a_sent, code], axis=1)
    a_got = exchange(a_sent.reshape(n_zy, pro, wide + LANES), ZY)
    codes = a_got[:, :1, wide : wide + 1].astype(F32)
    a_own = jnp.sum(a_got[:, :, :wide].astype(F32) * jnp.exp2(codes - 15.0), axis=0)

    def sum_b(token, orbitals, slab):
        b_part = cross_part(token, orbitals, slab)
        b_own = joint_sum(b_part.reshape(n_aa, lig, fit * pro), AA, aa)
        b_pair = b_own.astype(BF16)
        return b_own, in_order(b_pair, other(b_pair, "c"), "c").reshape(2 * lig, fit * pro)

    b_own, b_pair = together(sum_b, core, a_sent[:8, :LANES].astype(F32), ligand_orbitals, y)
    a_block, b_pair = spread(b_pair, a_own, n_zy)
    a_all = exchange(a_block, ZY).reshape(n_zy * pro, wide)
    pair = jnp.sum(
        jnp.transpose(a_own.reshape(pro, fit, lig), (1, 2, 0))
        * jnp.transpose(b_own.reshape(lig, fit, pro), (1, 0, 2)),
        axis=0,
    )
    pair_exchange = -pair / math.sqrt(fit)

    scale_ligand = 1.0 / math.sqrt(fit * pro_total)
    rows_b = nus // (2 * n_zy)

    def multiply_b(b_pair, slab):
        blocks, places = joint_gather(b_pair.reshape(2, lig, fit * pro), AA, aa)
        back_b = back_part(slab, blocks, places, scale_ligand, lig_total)
        keep, send = shared(back_b.reshape(n_z, nus // n_z, lig_total), ("z",), (n_z,))
        return keep + other(send, "c")

    back_b = together(multiply_b, core, b_pair, y)

    scale_protein = 1.0 / math.sqrt(fit * lig_total)
    rows = mus // n_aa
    back_a, sent = product(back_b, x_own, x_other, a_all, scale_protein, rows)

    def sum_back(back_b, sent):
        total = jnp.where(core == 0, back_b[-1], 0.0)
        for j, (first, second) in enumerate(zip(*halves((n_z,)))):
            total = total + joint(sent[j], ("z",), (n_z,), first, second).astype(F32)
        return direct_sum(total.reshape(n_yl * 2, rows_b, lig_total), ("yl", "c"), (n_yl, 2))

    ligand_back = together(sum_back, core, back_b, sent)
    back_a = exchange(back_a, AA)
    here, away = jnp.sum(back_a.astype(F32), axis=0)
    there = other(away + 0.0 * ligand_back[:1, :1], "c")
    here = here.reshape(rows, n_zy, 1, pro)
    there = there.reshape(rows, n_zy, 1, pro)
    protein_back = jnp.where(
        core == 0,
        jnp.concatenate([here, there], axis=2),
        jnp.concatenate([there, here], axis=2),
    ).reshape(rows, pro_total)
    return (pair_exchange, ligand_back, protein_back)


def solution(mesh):
    sizes = {"x": mesh.shape["aa"] // 2, "yh": 2, "z": mesh.shape["ba"] // 4, "yl": 2, "c": 2}
    fine = Mesh(mesh.devices.reshape([sizes[name] for name in AXES]), AXES)
    aa, ba = AA, ("z", "yl", "c")
    placed = (P(None, aa, ba), P(None, ba, aa), P(None, ba), P(None, aa))

    def body(*args):
        return on_device(*args, sizes=sizes)

    return jax.shard_map(
        body,
        mesh=fine,
        in_specs=placed,
        out_specs=(P(aa, ba), P(aa + ba, None), P(ba + aa, None)),
        check_vma=False,
    )
```
